128 devices in a mesh: gx: 2 (over core), gy: 64 (over z, y, x).
Axes of the slice: x: 4, y: 4, z: 4, core: 2. Of those that a mesh axis runs over, the one named last changes fastest.
Arguments:
- leaf_multipoles: bfloat16 [524288, 256], P(('gx', 'gy')), may hold values from -6 to 6
- m2m_ops: bfloat16 [8, 256, 256], replicated, may hold values from -0.125 to 0.125
- m2l_ops: bfloat16 [96, 256, 256], replicated, may hold values from -0.0546875 to 0.0546875
- l2l_ops: bfloat16 [8, 256, 256], replicated, may hold values from -0.375 to 0.375
- send_boxes: int32 [128, 3, 64, 128], P(('gx', 'gy')), may hold values from 0 to 511, as said below
- task_source: int32 [128, 96, 512], P(('gx', 'gy')), may hold values from 0 to 25087, as said below
- task_target: int32 [128, 96, 512], P(('gx', 'gy')), may hold values from 0 to 511, as said below
- task_count: int32 [128, 96], P(('gx', 'gy')), may hold values from 1 to 511, as said below
Outputs:
- leaf_local: float32 [524288, 256], P(('gx', 'gy'))
The draws below stay inside these ranges and needn't reach their ends.
Inputs may be any that keep to these rules, and one draw needn't show every extreme that they name: The 128 entries of send_boxes[s, a, j] are distinct. The entries of task_target[d, o] are distinct. `task_source`: no task of a device with gx index 0 reads rows 512 to 8703, and none of a device with gx index 1 reads the last 8192 rows. For devices d with (d // 64) even and p = d + 64, for every operator one of task_count[d, o] and task_count[p, o] exceeds 256, and the two sum to at most 512.
All inputs are finite; a program needn't handle non-finite values.
Results may differ from the reference program's by a relative error of at most 0.007.
Values may be sent and summed in bfloat16 or wider, within the bound.
A program may use at most 192 MiB of HBM per device.

```python
import jax
import jax.numpy as jnp
from jax import lax

COEFFS = 256
OPERATORS = 96
BOX_DEV = 512
GHOST_CAP = 128
HALF_SLOTS = 256
SLOTS = 512
PEERS = 128
PAIR_STRIDE = 64
ROWS = 25088
BOXES = 65536
LEAVES = 524288
N_GX = 2
N_GY = 64


def draw_send_boxes(key, part):
    key = jax.random.fold_in(key, 11)
    keys = jax.random.split(key, PEERS * 3 * N_GY)

    def pick_boxes(one_key):
        return jax.random.permutation(one_key, BOX_DEV)[:GHOST_CAP]
    picks = jax.vmap(pick_boxes)(keys)
    return picks.reshape(PEERS, 3, N_GY, GHOST_CAP).astype(jnp.int32)


def draw_task_source(key, part):
    key = jax.random.fold_in(key, 31)
    raw = jax.random.randint(key, (PEERS, OPERATORS, SLOTS), 0, ROWS)
    block = N_GY * GHOST_CAP
    column_ids = (jnp.arange(PEERS, dtype=jnp.int32) // N_GY)[:, None, None]
    left_edge = jnp.logical_and(column_ids == 0, jnp.logical_and(raw >= BOX_DEV, raw < BOX_DEV + block))
    right_edge = jnp.logical_and(column_ids == N_GX - 1, raw >= BOX_DEV + 2 * block)
    raw = jnp.where(left_edge, raw + block, raw)
    raw = jnp.where(right_edge, raw - block, raw)
    return raw.astype(jnp.int32)


def draw_task_target(key, part):
    key = jax.random.fold_in(key, 47)
    keys = jax.random.split(key, PEERS * OPERATORS)

    def pick_targets(one_key):
        return jax.random.permutation(one_key, BOX_DEV)[:SLOTS]
    picks = jax.vmap(pick_targets)(keys)
    return picks.reshape(PEERS, OPERATORS, SLOTS).astype(jnp.int32)


def draw_task_count(key, part):
    key = jax.random.fold_in(key, 23)
    first_key, second_key, third_key = jax.random.split(key, 3)
    heavy = jax.random.randint(first_key, (PEERS, OPERATORS), HALF_SLOTS + 1, SLOTS)
    heavy = heavy.at[:, 0].set(SLOTS - 1)
    light = jax.random.randint(second_key, (PEERS, OPERATORS), 1, SLOTS - heavy + 1)
    sides = jax.random.randint(third_key, (PEERS, OPERATORS), 0, 2)
    device_ids = jnp.arange(PEERS, dtype=jnp.int32)
    lower = device_ids // PAIR_STRIDE % 2 == 0
    base_ids = jnp.where(lower, device_ids, device_ids - PAIR_STRIDE)
    flags = jnp.where(lower, 0, 1)[:, None]
    heavy_here = sides[base_ids] == flags
    return jnp.where(heavy_here, heavy[base_ids], light[base_ids]).astype(jnp.int32)


def block_levels(stream_key, extent, cuts, least, largest):
    level = 1.0
    for position, shards_of in cuts:
        heights = jax.random.uniform(jax.random.fold_in(jax.random.fold_in(stream_key, 6), position), (shards_of,), jnp.float32, least / len(cuts), largest / len(cuts))
        level = level * jnp.repeat(jnp.exp(heights), extent[position] // shards_of).reshape((-1,) + (1,) * (len(extent) - 1 - position))
    return level


def scatter_about(rng, dims, spread, most, cuts=(), kind=jnp.bfloat16):
    values = jax.random.normal(rng, dims, jnp.float32) * spread
    if len(cuts) > 0:
        values = block_levels(rng, dims, cuts, -0.22, 0.18) * values
    return jnp.clip(values, min=-most, max=most).astype(kind)


def setup_inputs(seed: int = 0) -> dict:
    splits = jax.random.split(jax.random.key(seed), 9)
    return {
        "leaf_multipoles": scatter_about(splits[0], (LEAVES, COEFFS), 1.0, 6.0, ((0, 128),)),
        "m2m_ops": scatter_about(splits[1], (8, COEFFS, COEFFS), (8 * COEFFS) ** -0.5, 0.125),
        "m2l_ops": scatter_about(splits[2], (OPERATORS, COEFFS, COEFFS), (COEFFS * OPERATORS // 2) ** -0.5, 0.0546875),
        "l2l_ops": scatter_about(splits[3], (8, COEFFS, COEFFS), COEFFS ** -0.5, 0.375),
        "send_boxes": draw_send_boxes(jax.random.fold_in(splits[8], 71), 0),
        "task_source": draw_task_source(jax.random.fold_in(splits[8], 71), 0),
        "task_target": draw_task_target(jax.random.fold_in(splits[8], 71), 0),
        "task_count": draw_task_count(jax.random.fold_in(splits[8], 71), 0),
    }


def reference(leaf_multipoles, m2m_ops, m2l_ops, l2l_ops, send_boxes, task_source, task_target, task_count):
    leaves = leaf_multipoles.astype(jnp.float32).reshape(BOXES, 8, COEFFS)
    parents = jnp.einsum('bcp,cpq->bq', leaves, m2m_ops.astype(jnp.float32)).astype(jnp.bfloat16)
    device_ids = jnp.arange(PEERS, dtype=jnp.int32)[:, None, None]
    column_ids = device_ids // N_GY
    row_ids = device_ids % N_GY
    ghost_ref = jnp.maximum(task_source - BOX_DEV, 0)
    column_offset = ghost_ref // (N_GY * GHOST_CAP)
    source_row = (ghost_ref // GHOST_CAP) % N_GY
    ghost_slot = ghost_ref % GHOST_CAP
    owner_dev = jnp.clip((column_ids + column_offset - 1) * N_GY + source_row, 0, PEERS - 1).astype(jnp.int32)
    sent_box = send_boxes[owner_dev, 2 - column_offset, jnp.broadcast_to(row_ids, owner_dev.shape), ghost_slot]
    source_id = jnp.where(task_source < BOX_DEV, device_ids * BOX_DEV + task_source, owner_dev * BOX_DEV + sent_box).astype(jnp.int32)
    used_slot = jnp.arange(SLOTS, dtype=jnp.int32)[None, None, :] < task_count[:, :, None]
    target_id = jnp.where(used_slot, device_ids * BOX_DEV + task_target, BOXES).astype(jnp.int32)

    def per_operator(local_sum, op_index):
        gathered = parents[source_id[:, op_index, :].reshape(-1)]
        product = jnp.dot(gathered, m2l_ops[op_index], preferred_element_type=jnp.float32)
        added = jax.ops.segment_sum(product, target_id[:, op_index, :].reshape(-1), num_segments=BOXES + 1)
        return local_sum + added, None

    local_sum, _ = lax.scan(per_operator, jnp.zeros((BOXES + 1, COEFFS), jnp.float32), jnp.arange(OPERATORS, dtype=jnp.int32))
    parent_rounded = local_sum[:BOXES].astype(jnp.bfloat16)
    leaf_local = jnp.einsum('bp,cpq->bcq', parent_rounded.astype(jnp.float32), l2l_ops.astype(jnp.float32))
    return leaf_local.reshape(LEAVES, COEFFS)
```

```python
import jax
import jax.numpy as jnp
from jax import lax
from jax.experimental import pallas as pl
from jax.experimental.pallas import tpu as pltpu
from jax.sharding import PartitionSpec as P

CHUNK = 128


def m2l_kernel(ops, chunks_per_op, src_ref, nch_ref, tgt_ref, tab_hbm, op_hbm, out_ref,
               tab_ref, op_ref, xa_ref, xb_ref, acc_ref, list_ref, sem):
    coeffs = acc_ref.shape[1]
    boxes = acc_ref.shape[0]
    load_table = pltpu.make_async_copy(tab_hbm, tab_ref, sem.at[0])
    load_table.start()
    load_ops = pltpu.make_async_copy(op_hbm, op_ref, sem.at[1])
    load_ops.start()
    acc_ref[...] = jnp.zeros_like(acc_ref)

    def fill(o, pos):
        n = nch_ref[o]
        for c in range(chunks_per_op):
            list_ref[pos] = o * chunks_per_op + c
            pos = pos + jnp.where(c < n, 1, 0)
        return pos

    total = lax.fori_loop(0, ops, fill, 0)
    for i in range(8):
        list_ref[total + i] = ops * chunks_per_op
    load_table.wait()
    load_ops.wait()

    def gather(it, x_ref):
        for h in range(2):
            b = list_ref[2 * it + h] * CHUNK
            for i in range(CHUNK):
                x_ref[h * CHUNK + i] = tab_ref[src_ref[b + i]].astype(jnp.float32)

    def compute(it, x_ref):
        x2 = x_ref.reshape(4 * CHUNK, 128)
        ys, ps = [], []
        rows = lax.broadcasted_iota(jnp.int32, (boxes, CHUNK), 0)
        for h in range(2):
            ch = list_ref[2 * it + h]
            lo = x2[pl.ds(h * 2 * CHUNK, CHUNK, stride=2), :].astype(jnp.bfloat16)
            hi = x2[pl.ds(h * 2 * CHUNK + 1, CHUNK, stride=2), :].astype(jnp.bfloat16)
            xx = jnp.concatenate([lo, hi], axis=1)
            o = jnp.minimum(lax.div(ch, chunks_per_op), ops - 1)
            w = op_ref[pl.ds(pl.multiple_of(o * coeffs, coeffs), coeffs), :]
            ys.append(jnp.dot(xx, w, preferred_element_type=jnp.float32).astype(jnp.bfloat16))
            t = tgt_ref[pl.ds(ch, 1), :]
            ps.append(jnp.where(rows == t, 1.0, 0.0).astype(jnp.bfloat16))
        acc_ref[...] += jnp.dot(
            jnp.concatenate(ps, axis=1), jnp.concatenate(ys, axis=0),
            preferred_element_type=jnp.float32,
        )

    gather(0, xa_ref)

    @pl.loop(0, lax.div(total + 3, 4))
    def _(j):
        gather(2 * j + 1, xb_ref)
        compute(2 * j, xa_ref)
        gather(2 * j + 2, xa_ref)
        compute(2 * j + 1, xb_ref)

    out_ref[...] = acc_ref[...].astype(out_ref.dtype)


def m2l(table, src, tgt, counts, m2l_ops, boxes):
    ops, slots = src.shape
    coeffs = m2l_ops.shape[1]
    rows = table.shape[0]
    chunks_per_op = slots // CHUNK
    position = jnp.arange(slots, dtype=jnp.int32)[None, :]
    tgt = jnp.where(position < counts[:, None], tgt, -1)
    tgt = jnp.concatenate([tgt, jnp.full((8, slots), -1, jnp.int32)], 0)
    tgt = tgt.reshape(-1, CHUNK)
    src = jnp.concatenate([src.reshape(-1), jnp.zeros((slots,), jnp.int32)], 0)
    nch = (counts + (CHUNK - 1)) // CHUNK
    smem = pl.BlockSpec(memory_space=pltpu.SMEM)
    vmem = pl.BlockSpec(memory_space=pltpu.VMEM)
    anym = pl.BlockSpec(memory_space=pl.ANY)

    def kern(*refs):
        m2l_kernel(ops, chunks_per_op, *refs)

    return pl.pallas_call(
        kern,
        in_specs=[smem, smem, vmem, anym, anym],
        out_specs=vmem,
        out_shape=jax.ShapeDtypeStruct((boxes, coeffs), jnp.bfloat16),
        scratch_shapes=[
            pltpu.VMEM((rows, 2, 128), jnp.bfloat16),
            pltpu.VMEM((ops * coeffs, coeffs), jnp.bfloat16),
            pltpu.VMEM((2 * CHUNK, 2, 128), jnp.float32),
            pltpu.VMEM((2 * CHUNK, 2, 128), jnp.float32),
            pltpu.VMEM((boxes, coeffs), jnp.float32),
            pltpu.SMEM((ops * chunks_per_op + 16,), jnp.int32),
            pltpu.SemaphoreType.DMA((2,)),
        ],
        compiler_params=pltpu.CompilerParams(vmem_limit_bytes=50 << 20),
        name="m2l",
    )(src, nch, tgt, table, m2l_ops.reshape(ops * coeffs, coeffs))


def body(
    leaf_multipoles, m2m_ops, m2l_ops, l2l_ops, send_boxes, task_source, task_target, task_count
):
    coeff_count = leaf_multipoles.shape[1]
    box_count = leaf_multipoles.shape[0] // 8
    column = lax.axis_index("gx")
    leaves = leaf_multipoles.reshape(box_count, 8, coeff_count)
    parents = jnp.einsum("bcp,cpq->bq", leaves, m2m_ops, preferred_element_type=jnp.float32).astype(
        jnp.bfloat16
    )
    boxes = send_boxes[0]
    cap = boxes.shape[-1]
    peers = boxes.shape[1]
    other = jnp.where(column == 0, boxes[2], boxes[0])
    lists = jnp.stack([boxes[1], other], 0)
    outgoing = parents[lists]
    mixed = lax.all_to_all(outgoing, "gy", split_axis=1, concat_axis=1, tiled=True)
    crossed = lax.ppermute(mixed[1], "gx", [(0, 1), (1, 0)])
    table = jnp.concatenate(
        [parents, mixed[0].reshape(-1, coeff_count), crossed.reshape(-1, coeff_count)], 0
    )
    rows = table.shape[0]
    sources = task_source[0]
    block = peers * cap
    own = jnp.logical_and(sources >= box_count, sources < box_count + block)
    shifted = jnp.where(
        jnp.logical_and(column == 1, own), sources + block, sources - block
    )
    src = jnp.where(sources < box_count, sources, shifted)
    src = jnp.clip(src, 0, rows - 1)
    parent_rounded = m2l(
        table.reshape(rows, 2, 128), src, task_target[0], task_count[0], m2l_ops, box_count
    )
    leaf_local = jnp.einsum(
        "bp,cpq->bcq", parent_rounded, l2l_ops, preferred_element_type=jnp.float32
    )
    return leaf_local.reshape(-1, coeff_count)


def solution(mesh):
    return jax.shard_map(
        body,
        mesh=mesh,
        in_specs=(
            P(("gx", "gy"), None),
            P(),
            P(),
            P(),
            P(("gx", "gy"), None, None, None),
            P(("gx", "gy"), None, None),
            P(("gx", "gy"), None, None),
            P(("gx", "gy"), None),
        ),
        out_specs=P(("gx", "gy"), None),
        check_vma=False,
    )
```

```python
import jax
import jax.numpy as jnp
from jax import lax
from jax.experimental import pallas as pl
from jax.experimental.pallas import tpu as pltpu
from jax.sharding import PartitionSpec as P

CHUNK = 128
SIDE = 4
UNROLL = 16

INTERNAL = (0, 12, 4, 48, 28, 7, 49, 52, 29, 11, 6, 23, 45, 10, 22, 41, 46, 47)
PARENT = (-1, 0, 6, 7, 0, 6, 7, 4, 12, 10, 6, 7, 0, 29, 10, 12, 0, 29, 22, 23, 4, 22, 23, 7, 28, 41, 22, 11, 12, 28, 29, 47, 48, 49, 46, 47, 52, 41, 22, 23, 41, 45, 41, 47, 45, 29, 45, 46, 0, 48, 49, 48, 48, 52, 6, 7, 52, 41, 10, 11, 12, 49, 46, 47)
PLAN = (
    (0, 0, 0), (0, 0, 1), (1, 0, 0), (1, 0, 1), (1, 0, 16), (0, 12, 0), (0, 4, 0), (0, 48, 0),
    (0, 12, 1), (0, 4, 1), (0, 48, 1), (1, 12, 12), (1, 12, 8), (1, 12, 15), (1, 12, 60),
    (1, 4, 4), (1, 4, 20), (0, 28, 0), (0, 7, 0), (0, 49, 0), (1, 48, 48), (1, 48, 32),
    (1, 48, 51), (0, 52, 0), (0, 28, 1), (0, 7, 1), (0, 49, 1), (1, 28, 28), (1, 28, 24),
    (1, 7, 7), (1, 7, 3), (1, 7, 55), (0, 52, 1), (1, 49, 49), (1, 49, 33), (1, 49, 50),
    (1, 49, 61), (1, 52, 52), (1, 52, 36), (0, 29, 0), (1, 52, 53), (1, 52, 56), (0, 11, 0),
    (0, 29, 1), (0, 6, 0), (0, 23, 0), (1, 29, 29), (1, 29, 13), (1, 29, 17), (1, 29, 30),
    (0, 11, 1), (1, 11, 11), (1, 11, 27), (1, 11, 59), (0, 23, 1), (1, 23, 23), (1, 23, 19),
    (1, 23, 39), (0, 45, 0), (0, 6, 1), (1, 6, 6), (1, 6, 2), (1, 6, 5), (1, 6, 54), (0, 10, 0),
    (0, 45, 1), (0, 22, 0), (1, 45, 45), (1, 45, 44), (0, 41, 0), (0, 46, 0), (0, 22, 1),
    (1, 22, 22), (1, 22, 18), (1, 22, 21), (1, 22, 26), (1, 22, 38), (0, 10, 1), (1, 10, 10),
    (1, 10, 9), (1, 10, 14), (1, 10, 58), (0, 46, 1), (1, 46, 46), (1, 46, 34), (1, 46, 62),
    (0, 41, 1), (1, 41, 41), (1, 41, 25), (1, 41, 37), (0, 47, 0), (1, 41, 40), (1, 41, 42),
    (1, 41, 57), (0, 47, 1), (1, 47, 47), (1, 47, 31), (1, 47, 35), (1, 47, 43), (1, 47, 63),
)

PAD = 4


def list_layout():
    groups, order, pos = {}, [], {}
    for o in INTERNAL:
        members = [o] + [c for c in range(len(PARENT)) if PARENT[c] == o and c not in INTERNAL]
        start = len(order)
        for c in members:
            pos[c] = len(order)
            order.append(c)
        while len(order) % PAD:
            order.append(o)
        groups[o] = (start, len(order) - start)
    return groups, order, pos


def torus_add(base, offset, sign=1):
    parts = []
    for weight in (SIDE * SIDE, SIDE, 1):
        a = lax.rem(lax.div(base, weight), SIDE)
        b = (offset // weight) % SIDE
        if sign < 0:
            b = (SIDE - b) % SIDE
        parts.append(lax.rem(a + b, SIDE) * weight)
    return parts[0] + parts[1] + parts[2]


def comm_kernel(idx_in, own_block, ghost_own, ghost_other, *scratch):
    blocks = dict(zip(INTERNAL, (own_block,) + scratch[: len(INTERNAL) - 1]))
    scratch = scratch[len(INTERNAL) - 1 :]
    (land, idx, stage_own, stage_other, full_send, full_recv, idx_send, idx_recv, idx_load,
     own_send, own_recv, own_local, other_send, other_recv) = scratch
    groups, order, pos = list_layout()
    slot = {o: i for i, o in enumerate(INTERNAL)}
    peers = ghost_own.shape[0]
    cap = ghost_own.shape[1]
    half_rows = own_block.shape[0] // 2
    pair = 2 * cap
    me_u = lax.axis_index("gx")
    me_v = lax.axis_index("gy")
    ready = pltpu.get_barrier_semaphore()

    def mesh_id(offset, side=0, sign=1):
        column = me_u if side == 0 else 1 - me_u
        return (column, torus_add(me_v, offset, sign))

    near = [s * w for w in (SIDE * SIDE, SIDE, 1) for s in (1, SIDE - 1)]
    sends = [(o, 0) for o in sorted(set(near) | set(INTERNAL[1:]))]
    sends += [(o, 1) for o in [0] + near]
    for o, side in sends:
        pl.semaphore_signal(ready, inc=1, device_id=mesh_id(o, side, -1),
                            device_id_type=pl.DeviceIdType.MESH)
    pl.semaphore_wait(ready, len(sends))

    def remote(src, dst, send, recv, target):
        return pltpu.make_async_remote_copy(
            src_ref=src, dst_ref=dst, send_sem=send, recv_sem=recv, device_id=target,
            device_id_type=pl.DeviceIdType.MESH,
        )

    def full_copy(child, half):
        parent = PARENT[child]
        rows = pl.ds(half * half_rows, half_rows)
        step = torus_step(parent, child)
        k = (slot[child] - 1) * 2 + half
        return remote(blocks[parent].at[rows], blocks[child].at[rows], full_send.at[k],
                      full_recv.at[k], mesh_id(step))

    def idx_copy(o):
        start, n = groups[o]
        part = pl.ds(start * pair, n * pair)
        k = slot[o] - 1
        return remote(idx_in.at[part], land.at[part], idx_send.at[k], idx_recv.at[k], mesh_id(o))

    def idx_local(o):
        start, n = groups[o]
        part = pl.ds(start * pair, n * pair)
        src = idx_in if o == 0 else land
        return pltpu.make_async_copy(src.at[part], idx.at[part], idx_load.at[slot[o]])

    children = {o: [c for c in INTERNAL if PARENT[c] == o] for o in INTERNAL}
    loaded = set()
    for kind, o, arg in PLAN:
        if kind == 0:
            if o == 0:
                if arg == 0:
                    idx_local(0).start()
            else:
                full_copy(o, arg).wait_recv()
            for c in children[o]:
                full_copy(c, arg).start()
            if o == 0 and arg == 1:
                for c in INTERNAL[1:]:
                    idx_copy(c).start()
            if o != 0 and arg == 1:
                idx_copy(o).wait_recv()
                idx_local(o).start()
            continue
        if o not in loaded:
            idx_local(o).wait()
            loaded.add(o)
        block = blocks[o]
        p = pos[arg]
        for h, stage in ((0, stage_own), (1, stage_other)):

            def pick(g, carry, block=block, stage=stage, h=h, p=p):
                b = p * pair + h * cap + g * UNROLL
                rows = [block[idx[b + i]] for i in range(UNROLL)]
                for i in range(UNROLL):
                    stage[p, g * UNROLL + i] = rows[i]
                return carry

            lax.fori_loop(0, cap // UNROLL, pick, 0)
        owner = torus_add(me_v, o, -1)
        step = torus_step(o, arg) if arg != o else 0
        if arg == o:
            pltpu.make_async_copy(stage_own.at[p], ghost_own.at[owner], own_local).start()
        else:
            remote(stage_own.at[p], ghost_own.at[owner], own_send, own_recv, mesh_id(step)).start()
        remote(stage_other.at[p], ghost_other.at[owner], other_send, other_recv,
               mesh_id(step, 1)).start()

    here = (1 - me_u, me_v)
    inner = len(INTERNAL)
    part = ghost_own.at[pl.ds(0, peers - inner)]
    remote(part, part, own_send, own_recv, here).wait_recv()
    remote(ghost_other, ghost_other, other_send, other_recv, here).wait_recv()
    remote(part, part, own_send, own_recv, here).wait_send()
    remote(ghost_other, ghost_other, other_send, other_recv, here).wait_send()
    part = ghost_own.at[pl.ds(0, inner)]
    pltpu.make_async_copy(part, part, own_local).wait()
    for c in INTERNAL[1:]:
        idx_copy(c).wait_send()
        for half in range(2):
            full_copy(c, half).wait_send()


def torus_step(a, b):
    step = 0
    for weight in (SIDE * SIDE, SIDE, 1):
        step += (((b // weight) - (a // weight)) % SIDE) * weight
    return step


def exchange(parents, lists):
    _, peers, cap = lists.shape
    boxes, coeffs = parents.shape
    groups, order, pos = list_layout()
    me_v = lax.axis_index("gy")
    dest = jnp.stack([torus_add(me_v, o) for o in order])
    idx = jnp.transpose(lists, (1, 0, 2))[dest].reshape(-1)
    inner = len(INTERNAL)
    dma = pltpu.SemaphoreType.DMA
    anym = pl.BlockSpec(memory_space=pl.ANY)
    vmem = pl.BlockSpec(memory_space=pltpu.VMEM)
    ghost = jax.ShapeDtypeStruct((peers, cap, 2, coeffs // 2), parents.dtype)
    return pl.pallas_call(
        comm_kernel,
        in_specs=[vmem, vmem],
        out_specs=[anym, anym],
        out_shape=[ghost, ghost],
        scratch_shapes=[pltpu.VMEM((boxes, 2, coeffs // 2), parents.dtype)] * (inner - 1)
        + [
            pltpu.VMEM(idx.shape, jnp.int32),
            pltpu.SMEM(idx.shape, jnp.int32),
            pltpu.VMEM((len(order), cap, 2, coeffs // 2), parents.dtype),
            pltpu.VMEM((len(order), cap, 2, coeffs // 2), parents.dtype),
            dma((2 * inner - 2,)),
            dma((2 * inner - 2,)),
            dma((inner - 1,)),
            dma((inner - 1,)),
            dma((inner,)),
            dma, dma, dma, dma, dma,
        ],
        compiler_params=pltpu.CompilerParams(
            collective_id=0, has_side_effects=True, vmem_limit_bytes=40 << 20
        ),
        name="exchange",
    )(idx, parents.reshape(boxes, 2, coeffs // 2))


def m2l_kernel(ops, chunks_per_op, src_ref, nch_ref, tgt_ref, par_hbm, own_hbm, other_hbm, op_hbm, out_ref,
               tab_ref, op_ref, xa_ref, xb_ref, acc_ref, list_ref, sem):
    coeffs = acc_ref.shape[1]
    boxes = acc_ref.shape[0]
    loads = []
    first = 0
    for i, part in enumerate((par_hbm, own_hbm, other_hbm)):
        n = part.shape[0]
        loads.append(pltpu.make_async_copy(part, tab_ref.at[pl.ds(first, n)], sem.at[1 + i]))
        loads[-1].start()
        first += n
    load_ops = pltpu.make_async_copy(op_hbm, op_ref, sem.at[0])
    load_ops.start()
    acc_ref[...] = jnp.zeros_like(acc_ref)

    def fill(o, pos):
        n = nch_ref[o]
        for c in range(chunks_per_op):
            list_ref[pos] = o * chunks_per_op + c
            pos = pos + jnp.where(c < n, 1, 0)
        return pos

    total = lax.fori_loop(0, ops, fill, 0)
    for i in range(8):
        list_ref[total + i] = ops * chunks_per_op
    for load in loads:
        load.wait()
    load_ops.wait()

    def gather(it, x_ref):
        for h in range(2):
            b = list_ref[2 * it + h] * CHUNK
            for i in range(CHUNK):
                x_ref[h * CHUNK + i] = tab_ref[src_ref[b + i]].astype(jnp.float32)

    def compute(it, x_ref):
        x2 = x_ref.reshape(4 * CHUNK, 128)
        ys, ps = [], []
        rows = lax.broadcasted_iota(jnp.int32, (boxes, CHUNK), 0)
        for h in range(2):
            ch = list_ref[2 * it + h]
            lo = x2[pl.ds(h * 2 * CHUNK, CHUNK, stride=2), :].astype(jnp.bfloat16)
            hi = x2[pl.ds(h * 2 * CHUNK + 1, CHUNK, stride=2), :].astype(jnp.bfloat16)
            xx = jnp.concatenate([lo, hi], axis=1)
            o = jnp.minimum(lax.div(ch, chunks_per_op), ops - 1)
            w = op_ref[pl.ds(pl.multiple_of(o * coeffs, coeffs), coeffs), :]
            ys.append(jnp.dot(xx, w, preferred_element_type=jnp.float32).astype(jnp.bfloat16))
            t = tgt_ref[pl.ds(ch, 1), :]
            ps.append(jnp.where(rows == t, 1.0, 0.0).astype(jnp.bfloat16))
        acc_ref[...] += jnp.dot(
            jnp.concatenate(ps, axis=1), jnp.concatenate(ys, axis=0),
            preferred_element_type=jnp.float32,
        )

    gather(0, xa_ref)

    @pl.loop(0, lax.div(total + 3, 4))
    def _(j):
        gather(2 * j + 1, xb_ref)
        compute(2 * j, xa_ref)
        gather(2 * j + 2, xa_ref)
        compute(2 * j + 1, xb_ref)

    out_ref[...] = acc_ref[...].astype(out_ref.dtype)


def m2l(parents, ghosts, src, tgt, counts, m2l_ops, boxes):
    ops, slots = src.shape
    coeffs = m2l_ops.shape[1]
    own, other = (g.reshape(-1, 2, coeffs // 2) for g in ghosts)
    rows = parents.shape[0] + own.shape[0] + other.shape[0]
    chunks_per_op = slots // CHUNK
    position = jnp.arange(slots, dtype=jnp.int32)[None, :]
    tgt = jnp.where(position < counts[:, None], tgt, -1)
    tgt = jnp.concatenate([tgt, jnp.full((8, slots), -1, jnp.int32)], 0)
    tgt = tgt.reshape(-1, CHUNK)
    src = jnp.concatenate([src.reshape(-1), jnp.zeros((slots,), jnp.int32)], 0)
    nch = (counts + (CHUNK - 1)) // CHUNK
    smem = pl.BlockSpec(memory_space=pltpu.SMEM)
    vmem = pl.BlockSpec(memory_space=pltpu.VMEM)
    anym = pl.BlockSpec(memory_space=pl.ANY)

    def kern(*refs):
        m2l_kernel(ops, chunks_per_op, *refs)

    return pl.pallas_call(
        kern,
        in_specs=[smem, smem, vmem, anym, anym, anym, anym],
        out_specs=vmem,
        out_shape=jax.ShapeDtypeStruct((boxes, coeffs), jnp.bfloat16),
        scratch_shapes=[
            pltpu.VMEM((rows, 2, 128), jnp.bfloat16),
            pltpu.VMEM((ops * coeffs, coeffs), jnp.bfloat16),
            pltpu.VMEM((2 * CHUNK, 2, 128), jnp.float32),
            pltpu.VMEM((2 * CHUNK, 2, 128), jnp.float32),
            pltpu.VMEM((boxes, coeffs), jnp.float32),
            pltpu.SMEM((ops * chunks_per_op + 16,), jnp.int32),
            pltpu.SemaphoreType.DMA((4,)),
        ],
        compiler_params=pltpu.CompilerParams(vmem_limit_bytes=50 << 20),
        name="m2l",
    )(src, nch, tgt, parents, own, other, m2l_ops.reshape(ops * coeffs, coeffs))


def body(
    leaf_multipoles, m2m_ops, m2l_ops, l2l_ops, send_boxes, task_source, task_target, task_count
):
    coeff_count = leaf_multipoles.shape[1]
    box_count = leaf_multipoles.shape[0] // 8
    column = lax.axis_index("gx")
    leaves = leaf_multipoles.reshape(box_count, 8, coeff_count)
    parents = jnp.einsum("bcp,cpq->bq", leaves, m2m_ops, preferred_element_type=jnp.float32).astype(
        jnp.bfloat16
    )
    boxes = send_boxes[0]
    cap = boxes.shape[-1]
    peers = boxes.shape[1]
    other = jnp.where(column == 0, boxes[2], boxes[0])
    lists = jnp.stack([boxes[1], other], 0)
    ghosts = exchange(parents, lists)
    rows = box_count + 2 * peers * cap
    sources = task_source[0]
    block = peers * cap
    own = jnp.logical_and(sources >= box_count, sources < box_count + block)
    shifted = jnp.where(
        jnp.logical_and(column == 1, own), sources + block, sources - block
    )
    src = jnp.where(sources < box_count, sources, shifted)
    src = jnp.clip(src, 0, rows - 1)
    parent_rounded = m2l(
        parents.reshape(box_count, 2, -1), ghosts, src, task_target[0], task_count[0], m2l_ops, box_count
    )
    leaf_local = jnp.einsum(
        "bp,cpq->bcq", parent_rounded, l2l_ops, preferred_element_type=jnp.float32
    )
    return leaf_local.reshape(-1, coeff_count)


def solution(mesh):
    return jax.shard_map(
        body,
        mesh=mesh,
        in_specs=(
            P(("gx", "gy"), None),
            P(),
            P(),
            P(),
            P(("gx", "gy"), None, None, None),
            P(("gx", "gy"), None, None),
            P(("gx", "gy"), None, None),
            P(("gx", "gy"), None),
        ),
        out_specs=P(("gx", "gy"), None),
        check_vma=False,
    )
```

```python
import jax
import jax.numpy as jnp
from jax import lax
from jax.experimental import pallas as pl
from jax.experimental.pallas import tpu as pltpu
from jax.sharding import PartitionSpec as P

CHUNK = 128
BATCH = 4
SIDE = 4
UNROLL = 16

INTERNAL = (0, 12, 4, 48, 28, 7, 49, 52, 29, 11, 6, 23, 45, 10, 22, 41, 46, 47)
PARENT = (-1, 0, 6, 7, 0, 6, 7, 4, 12, 10, 6, 7, 0, 29, 10, 12, 0, 29, 22, 23, 4, 22, 23, 7, 28, 41, 22, 11, 12, 28, 29, 47, 48, 49, 46, 47, 52, 41, 22, 23, 41, 45, 41, 47, 45, 29, 45, 46, 0, 48, 49, 48, 48, 52, 6, 7, 52, 41, 10, 11, 12, 49, 46, 47)
PLAN = (
    (0, 0, 0), (0, 0, 1), (1, 0, 0), (1, 0, 1), (1, 0, 16), (0, 12, 0), (0, 4, 0), (0, 48, 0),
    (0, 12, 1), (0, 4, 1), (0, 48, 1), (1, 12, 12), (1, 12, 8), (1, 12, 15), (1, 12, 60),
    (1, 4, 4), (1, 4, 20), (0, 28, 0), (0, 7, 0), (0, 49, 0), (1, 48, 48), (1, 48, 32),
    (1, 48, 51), (0, 52, 0), (0, 28, 1), (0, 7, 1), (0, 49, 1), (1, 28, 28), (1, 28, 24),
    (1, 7, 7), (1, 7, 3), (1, 7, 55), (0, 52, 1), (1, 49, 49), (1, 49, 33), (1, 49, 50),
    (1, 49, 61), (1, 52, 52), (1, 52, 36), (0, 29, 0), (1, 52, 53), (1, 52, 56), (0, 11, 0),
    (0, 29, 1), (0, 6, 0), (0, 23, 0), (1, 29, 29), (1, 29, 13), (1, 29, 17), (1, 29, 30),
    (0, 11, 1), (1, 11, 11), (1, 11, 27), (1, 11, 59), (0, 23, 1), (1, 23, 23), (1, 23, 19),
    (1, 23, 39), (0, 45, 0), (0, 6, 1), (1, 6, 6), (1, 6, 2), (1, 6, 5), (1, 6, 54), (0, 10, 0),
    (0, 45, 1), (0, 22, 0), (1, 45, 45), (1, 45, 44), (0, 41, 0), (0, 46, 0), (0, 22, 1),
    (1, 22, 22), (1, 22, 18), (1, 22, 21), (1, 22, 26), (1, 22, 38), (0, 10, 1), (1, 10, 10),
    (1, 10, 9), (1, 10, 14), (1, 10, 58), (0, 46, 1), (1, 46, 46), (1, 46, 34), (1, 46, 62),
    (0, 41, 1), (1, 41, 41), (1, 41, 25), (1, 41, 37), (0, 47, 0), (1, 41, 40), (1, 41, 42),
    (1, 41, 57), (0, 47, 1), (1, 47, 47), (1, 47, 31), (1, 47, 35), (1, 47, 43), (1, 47, 63),
)

PAD = 4


def list_layout():
    groups, order, pos = {}, [], {}
    for o in INTERNAL:
        members = [o] + [c for c in range(len(PARENT)) if PARENT[c] == o and c not in INTERNAL]
        start = len(order)
        for c in members:
            pos[c] = len(order)
            order.append(c)
        while len(order) % PAD:
            order.append(o)
        groups[o] = (start, len(order) - start)
    return groups, order, pos


def torus_add(base, offset, sign=1):
    parts = []
    for weight in (SIDE * SIDE, SIDE, 1):
        a = lax.rem(lax.div(base, weight), SIDE)
        b = (offset // weight) % SIDE
        if sign < 0:
            b = (SIDE - b) % SIDE
        parts.append(lax.rem(a + b, SIDE) * weight)
    return parts[0] + parts[1] + parts[2]


def comm_kernel(peers, idx_in, own_block, table, *scratch):
    blocks = dict(zip(INTERNAL, (own_block,) + scratch[: len(INTERNAL) - 1]))
    scratch = scratch[len(INTERNAL) - 1 :]
    (land, idx, stage_own, stage_other, full_send, full_recv, idx_send, idx_recv, idx_load,
     own_send, own_recv, own_local, other_send, other_recv, self_local) = scratch
    groups, order, pos = list_layout()
    slot = {o: i for i, o in enumerate(INTERNAL)}
    cap = stage_own.shape[1]
    boxes = own_block.shape[0]
    half_rows = own_block.shape[0] // 2
    pair = 2 * cap
    me_u = lax.axis_index("gx")
    me_v = lax.axis_index("gy")
    ready = pltpu.get_barrier_semaphore()

    def mesh_id(offset, side=0, sign=1):
        column = me_u if side == 0 else 1 - me_u
        return (column, torus_add(me_v, offset, sign))

    near = [s * w for w in (SIDE * SIDE, SIDE, 1) for s in (1, SIDE - 1)]
    sends = [(o, 0) for o in sorted(set(near) | set(INTERNAL[1:]))]
    sends += [(o, 1) for o in [0] + near]
    for o, side in sends:
        pl.semaphore_signal(ready, inc=1, device_id=mesh_id(o, side, -1),
                            device_id_type=pl.DeviceIdType.MESH)
    pl.semaphore_wait(ready, len(sends))

    def ghost(side, owner, count=1):
        first = boxes + (side * peers + owner) * cap
        return table.at[pl.ds(first, count * cap)]

    def remote(src, dst, send, recv, target):
        return pltpu.make_async_remote_copy(
            src_ref=src, dst_ref=dst, send_sem=send, recv_sem=recv, device_id=target,
            device_id_type=pl.DeviceIdType.MESH,
        )

    def full_copy(child, half):
        parent = PARENT[child]
        rows = pl.ds(half * half_rows, half_rows)
        step = torus_step(parent, child)
        k = (slot[child] - 1) * 2 + half
        return remote(blocks[parent].at[rows], blocks[child].at[rows], full_send.at[k],
                      full_recv.at[k], mesh_id(step))

    def idx_copy(o):
        start, n = groups[o]
        part = pl.ds(start * pair, n * pair)
        k = slot[o] - 1
        return remote(idx_in.at[part], land.at[part], idx_send.at[k], idx_recv.at[k], mesh_id(o))

    def idx_local(o):
        start, n = groups[o]
        part = pl.ds(start * pair, n * pair)
        src = idx_in if o == 0 else land
        return pltpu.make_async_copy(src.at[part], idx.at[part], idx_load.at[slot[o]])

    self_copy = pltpu.make_async_copy(own_block, table.at[pl.ds(0, boxes)], self_local)
    self_copy.start()
    children = {o: [c for c in INTERNAL if PARENT[c] == o] for o in INTERNAL}
    loaded = set()
    for kind, o, arg in PLAN:
        if kind == 0:
            if o == 0:
                if arg == 0:
                    idx_local(0).start()
            else:
                full_copy(o, arg).wait_recv()
            for c in children[o]:
                full_copy(c, arg).start()
            if o == 0 and arg == 1:
                for c in INTERNAL[1:]:
                    idx_copy(c).start()
            if o != 0 and arg == 1:
                idx_copy(o).wait_recv()
                idx_local(o).start()
            continue
        if o not in loaded:
            idx_local(o).wait()
            loaded.add(o)
        block = blocks[o]
        p = pos[arg]
        for h, stage in ((0, stage_own), (1, stage_other)):

            def pick(g, carry, block=block, stage=stage, h=h, p=p):
                b = p * pair + h * cap + g * UNROLL
                rows = [block[idx[b + i]] for i in range(UNROLL)]
                for i in range(UNROLL):
                    stage[p, g * UNROLL + i] = rows[i]
                return carry

            lax.fori_loop(0, cap // UNROLL, pick, 0)
        owner = torus_add(me_v, o, -1)
        step = torus_step(o, arg) if arg != o else 0
        if arg == o:
            pltpu.make_async_copy(stage_own.at[p], ghost(0, owner), own_local).start()
        else:
            remote(stage_own.at[p], ghost(0, owner), own_send, own_recv, mesh_id(step)).start()
        remote(stage_other.at[p], ghost(1, owner), other_send, other_recv,
               mesh_id(step, 1)).start()

    here = (1 - me_u, me_v)
    inner = len(INTERNAL)
    part = ghost(0, 0, peers - inner)
    side = ghost(1, 0, peers)
    remote(part, part, own_send, own_recv, here).wait_recv()
    remote(side, side, other_send, other_recv, here).wait_recv()
    remote(part, part, own_send, own_recv, here).wait_send()
    remote(side, side, other_send, other_recv, here).wait_send()
    part = ghost(0, 0, inner)
    pltpu.make_async_copy(part, part, own_local).wait()
    self_copy.wait()
    for c in INTERNAL[1:]:
        idx_copy(c).wait_send()
        for half in range(2):
            full_copy(c, half).wait_send()


def torus_step(a, b):
    step = 0
    for weight in (SIDE * SIDE, SIDE, 1):
        step += (((b // weight) - (a // weight)) % SIDE) * weight
    return step


def exchange(parents, lists):
    _, peers, cap = lists.shape
    boxes, coeffs = parents.shape
    groups, order, pos = list_layout()
    me_v = lax.axis_index("gy")
    dest = jnp.stack([torus_add(me_v, o) for o in order])
    idx = jnp.transpose(lists, (1, 0, 2))[dest].reshape(-1)
    inner = len(INTERNAL)
    dma = pltpu.SemaphoreType.DMA
    vmem = pl.BlockSpec(memory_space=pltpu.VMEM)

    def kern(*refs):
        comm_kernel(peers, *refs)

    return pl.pallas_call(
        kern,
        in_specs=[vmem, vmem],
        out_specs=vmem,
        out_shape=pltpu.VMEM((boxes + 2 * peers * cap, 2, coeffs // 2), parents.dtype),
        scratch_shapes=[pltpu.VMEM((boxes, 2, coeffs // 2), parents.dtype)] * (inner - 1)
        + [
            pltpu.VMEM(idx.shape, jnp.int32),
            pltpu.SMEM(idx.shape, jnp.int32),
            pltpu.VMEM((len(order), cap, 2, coeffs // 2), parents.dtype),
            pltpu.VMEM((len(order), cap, 2, coeffs // 2), parents.dtype),
            dma((2 * inner - 2,)),
            dma((2 * inner - 2,)),
            dma((inner - 1,)),
            dma((inner - 1,)),
            dma((inner,)),
            dma, dma, dma, dma, dma, dma,
        ],
        compiler_params=pltpu.CompilerParams(
            collective_id=0, has_side_effects=True, vmem_limit_bytes=20 << 20
        ),
        name="exchange",
    )(idx, parents.reshape(boxes, 2, coeffs // 2))


def m2l_kernel(ops, chunks_per_op, src_ref, nch_ref, tgt_ref, tab_ref, op_ref, out_ref,
               x_ref, y_ref, acc_ref, list_ref):
    boxes, coeffs = acc_ref.shape
    stride = src_ref.shape[0] // CHUNK
    empty = ops * chunks_per_op
    acc_ref[...] = jnp.zeros_like(acc_ref)
    y_ref[...] = jnp.zeros_like(y_ref)

    def fill(o, pos):
        n = nch_ref[o]
        for c in range(chunks_per_op):
            list_ref[pos] = o * chunks_per_op + c
            pos = pos + jnp.where(c < n, 1, 0)
        return pos

    for i in range(BATCH):
        list_ref[i] = empty
    total = lax.fori_loop(0, ops, fill, BATCH)
    for i in range(3 * BATCH):
        list_ref[total + i] = empty

    def gather(it):
        for h in range(BATCH):
            ch = list_ref[BATCH * it + h]
            for i in range(CHUNK):
                s = src_ref.at[pl.ds(i * stride, stride)][ch]
                x_ref[h * CHUNK + i] = tab_ref[s].astype(jnp.float32)

    def translate(it):
        x2 = x_ref.reshape(2 * BATCH * CHUNK, x_ref.shape[2])
        for h in range(BATCH):
            ch = list_ref[BATCH * it + h]
            first = 2 * CHUNK * h
            lo = x2[pl.ds(first, CHUNK, stride=2), :].astype(jnp.bfloat16)
            hi = x2[pl.ds(first + 1, CHUNK, stride=2), :].astype(jnp.bfloat16)
            o = jnp.minimum(lax.div(ch, chunks_per_op), ops - 1)
            w = op_ref[pl.ds(pl.multiple_of(o * coeffs, coeffs), coeffs), :]
            y_ref[h * CHUNK : (h + 1) * CHUNK, :] = jnp.dot(
                jnp.concatenate([lo, hi], axis=1), w, preferred_element_type=jnp.float32
            ).astype(jnp.bfloat16)

    def scatter(it):
        rows = lax.broadcasted_iota(jnp.int32, (boxes, CHUNK), 0)
        ps = []
        for h in range(BATCH):
            t = tgt_ref[pl.ds(list_ref[BATCH * it + h], 1), :]
            ps.append(jnp.where(rows == t, 1.0, 0.0).astype(jnp.bfloat16))
        acc_ref[...] += jnp.dot(
            jnp.concatenate(ps, axis=1), y_ref[...], preferred_element_type=jnp.float32
        )

    gather(1)

    @pl.loop(1, lax.div(total + BATCH - 1, BATCH) + 1)
    def _(j):
        scatter(j - 1)
        translate(j)
        gather(j + 1)

    out_ref[...] = acc_ref[...].astype(out_ref.dtype)


def m2l(table, src, tgt, counts, m2l_ops, boxes):
    ops, slots = src.shape
    coeffs = m2l_ops.shape[1]
    chunks_per_op = slots // CHUNK
    chunks = ops * chunks_per_op
    position = jnp.arange(slots, dtype=jnp.int32)[None, :]
    tgt = jnp.where(position < counts[:, None], tgt, -1)
    tgt = jnp.pad(tgt.reshape(-1, CHUNK), ((0, 8), (0, 0)), constant_values=-1)
    stride = -(-(chunks + 1) // 128) * 128
    src = jnp.pad(src.reshape(-1, CHUNK).T, ((0, 0), (0, stride - chunks))).reshape(-1)
    nch = (counts + (CHUNK - 1)) // CHUNK
    smem = pl.BlockSpec(memory_space=pltpu.SMEM)
    vmem = pl.BlockSpec(memory_space=pltpu.VMEM)

    def kern(*refs):
        m2l_kernel(ops, chunks_per_op, *refs)

    return pl.pallas_call(
        kern,
        in_specs=[smem, smem, vmem, vmem, vmem],
        out_specs=vmem,
        out_shape=jax.ShapeDtypeStruct((boxes, coeffs), jnp.bfloat16),
        scratch_shapes=[
            pltpu.VMEM((BATCH * CHUNK, 2, coeffs // 2), jnp.float32),
            pltpu.VMEM((BATCH * CHUNK, coeffs), jnp.bfloat16),
            pltpu.VMEM((boxes, coeffs), jnp.float32),
            pltpu.SMEM((chunks + 4 * BATCH,), jnp.int32),
        ],
        compiler_params=pltpu.CompilerParams(vmem_limit_bytes=8 << 20),
        name="m2l",
    )(
        src, nch, tgt,
        pltpu.with_memory_space_constraint(table, pltpu.VMEM),
        pltpu.with_memory_space_constraint(m2l_ops.reshape(ops * coeffs, coeffs), pltpu.VMEM),
    )


def body(
    leaf_multipoles, m2m_ops, m2l_ops, l2l_ops, send_boxes, task_source, task_target, task_count
):
    coeff_count = leaf_multipoles.shape[1]
    box_count = leaf_multipoles.shape[0] // 8
    column = lax.axis_index("gx")
    leaves = leaf_multipoles.reshape(box_count, 8, coeff_count)
    parents = jnp.einsum("bcp,cpq->bq", leaves, m2m_ops, preferred_element_type=jnp.float32).astype(
        jnp.bfloat16
    )
    boxes = send_boxes[0]
    cap = boxes.shape[-1]
    peers = boxes.shape[1]
    other = jnp.where(column == 0, boxes[2], boxes[0])
    lists = jnp.stack([boxes[1], other], 0)
    table = exchange(parents, lists)
    rows = table.shape[0]
    sources = task_source[0]
    block = peers * cap
    own = jnp.logical_and(sources >= box_count, sources < box_count + block)
    shifted = jnp.where(
        jnp.logical_and(column == 1, own), sources + block, sources - block
    )
    src = jnp.where(sources < box_count, sources, shifted)
    src = jnp.clip(src, 0, rows - 1)
    parent_rounded = m2l(
        table, src, task_target[0], task_count[0], m2l_ops, box_count
    )
    leaf_local = jnp.einsum(
        "bp,cpq->bcq", parent_rounded, l2l_ops, preferred_element_type=jnp.float32
    )
    return leaf_local.reshape(-1, coeff_count)


def solution(mesh):
    return jax.shard_map(
        body,
        mesh=mesh,
        in_specs=(
            P(("gx", "gy"), None),
            P(),
            P(),
            P(),
            P(("gx", "gy"), None, None, None),
            P(("gx", "gy"), None, None),
            P(("gx", "gy"), None, None),
            P(("gx", "gy"), None),
        ),
        out_specs=P(("gx", "gy"), None),
        check_vma=False,
    )
```

```python
import jax
import jax.numpy as jnp
from jax import lax
from jax.experimental import pallas as pl
from jax.experimental.pallas import tpu as pltpu
from jax.sharding import PartitionSpec as P

CHUNK = 128
BATCH = 4
SIDE = 4
UNROLL = 32

INTERNAL = (0, 12, 4, 48, 28, 7, 49, 52, 29, 11, 6, 23, 45, 10, 22, 41, 46, 47)
PARENT = (-1, 0, 6, 7, 0, 6, 7, 4, 12, 10, 6, 7, 0, 29, 10, 12, 0, 29, 22, 23, 4, 22, 23, 7, 28, 41, 22, 11, 12, 28, 29, 47, 48, 49, 46, 47, 52, 41, 22, 23, 41, 45, 41, 47, 45, 29, 45, 46, 0, 48, 49, 48, 48, 52, 6, 7, 52, 41, 10, 11, 12, 49, 46, 47)
PLAN = (
    (0, 0, 0), (0, 0, 1), (1, 0, 0), (1, 0, 1), (1, 0, 16), (0, 12, 0), (0, 4, 0), (0, 48, 0),
    (0, 12, 1), (0, 4, 1), (0, 48, 1), (1, 12, 12), (1, 12, 8), (1, 12, 15), (1, 12, 60),
    (1, 4, 4), (1, 4, 20), (0, 28, 0), (0, 7, 0), (0, 49, 0), (1, 48, 48), (1, 48, 32),
    (1, 48, 51), (0, 52, 0), (0, 28, 1), (0, 7, 1), (0, 49, 1), (1, 28, 28), (1, 28, 24),
    (1, 7, 7), (1, 7, 3), (1, 7, 55), (0, 52, 1), (1, 49, 49), (1, 49, 33), (1, 49, 50),
    (1, 49, 61), (1, 52, 52), (1, 52, 36), (0, 29, 0), (1, 52, 53), (1, 52, 56), (0, 11, 0),
    (0, 29, 1), (0, 6, 0), (0, 23, 0), (1, 29, 29), (1, 29, 13), (1, 29, 17), (1, 29, 30),
    (0, 11, 1), (1, 11, 11), (1, 11, 27), (1, 11, 59), (0, 23, 1), (1, 23, 23), (1, 23, 19),
    (1, 23, 39), (0, 45, 0), (0, 6, 1), (1, 6, 6), (1, 6, 2), (1, 6, 5), (1, 6, 54), (0, 10, 0),
    (0, 45, 1), (0, 22, 0), (1, 45, 45), (1, 45, 44), (0, 41, 0), (0, 46, 0), (0, 22, 1),
    (1, 22, 22), (1, 22, 18), (1, 22, 21), (1, 22, 26), (1, 22, 38), (0, 10, 1), (1, 10, 10),
    (1, 10, 9), (1, 10, 14), (1, 10, 58), (0, 46, 1), (1, 46, 46), (1, 46, 34), (1, 46, 62),
    (0, 41, 1), (1, 41, 41), (1, 41, 25), (1, 41, 37), (0, 47, 0), (1, 41, 40), (1, 41, 42),
    (1, 41, 57), (0, 47, 1), (1, 47, 47), (1, 47, 31), (1, 47, 35), (1, 47, 43), (1, 47, 63),
)

PAD = 4


def list_layout():
    groups, order, pos = {}, [], {}
    for o in INTERNAL:
        members = [o] + [c for c in range(len(PARENT)) if PARENT[c] == o and c not in INTERNAL]
        start = len(order)
        for c in members:
            pos[c] = len(order)
            order.append(c)
        while len(order) % PAD:
            order.append(o)
        groups[o] = (start, len(order) - start)
    return groups, order, pos


def torus_add(base, offset, sign=1):
    parts = []
    for weight in (SIDE * SIDE, SIDE, 1):
        a = lax.rem(lax.div(base, weight), SIDE)
        b = (offset // weight) % SIDE
        if sign < 0:
            b = (SIDE - b) % SIDE
        parts.append(lax.rem(a + b, SIDE) * weight)
    return parts[0] + parts[1] + parts[2]


def comm_kernel(peers, idx_in, own_block, ops_in, src_in, tgt_in, table, ops_out, src_out, tgt_out, *scratch):
    blocks = dict(zip(INTERNAL, (own_block,) + scratch[: len(INTERNAL) - 1]))
    scratch = scratch[len(INTERNAL) - 1 :]
    (land, idx, stage_own, stage_other, full_send, full_recv, idx_send, idx_recv, idx_load,
     own_send, own_recv, own_local, other_send, other_recv, keep) = scratch
    groups, order, pos = list_layout()
    slot = {o: i for i, o in enumerate(INTERNAL)}
    cap = stage_own.shape[1]
    boxes = own_block.shape[0]
    half_rows = own_block.shape[0] // 2
    pair = 2 * cap
    me_u = lax.axis_index("gx")
    me_v = lax.axis_index("gy")
    ready = pltpu.get_barrier_semaphore()

    def mesh_id(offset, side=0, sign=1):
        column = me_u if side == 0 else 1 - me_u
        return (column, torus_add(me_v, offset, sign))

    near = [s * w for w in (SIDE * SIDE, SIDE, 1) for s in (1, SIDE - 1)]
    sends = [(o, 0) for o in sorted(set(near) | set(INTERNAL[1:]))]
    sends += [(o, 1) for o in [0] + near]
    for o, side in sends:
        pl.semaphore_signal(ready, inc=1, device_id=mesh_id(o, side, -1),
                            device_id_type=pl.DeviceIdType.MESH)
    pl.semaphore_wait(ready, len(sends))

    def ghost(side, owner, count=1):
        first = boxes + (side * peers + owner) * cap
        return table.at[pl.ds(first, count * cap)]

    def remote(src, dst, send, recv, target):
        return pltpu.make_async_remote_copy(
            src_ref=src, dst_ref=dst, send_sem=send, recv_sem=recv, device_id=target,
            device_id_type=pl.DeviceIdType.MESH,
        )

    def full_copy(child, half):
        parent = PARENT[child]
        rows = pl.ds(half * half_rows, half_rows)
        step = torus_step(parent, child)
        k = (slot[child] - 1) * 2 + half
        return remote(blocks[parent].at[rows], blocks[child].at[rows], full_send.at[k],
                      full_recv.at[k], mesh_id(step))

    def idx_copy(o):
        start, n = groups[o]
        part = pl.ds(start * pair, n * pair)
        k = slot[o] - 1
        return remote(idx_in.at[part], land.at[part], idx_send.at[k], idx_recv.at[k], mesh_id(o))

    def idx_local(o):
        start, n = groups[o]
        part = pl.ds(start * pair, n * pair)
        src = idx_in if o == 0 else land
        return pltpu.make_async_copy(src.at[part], idx.at[part], idx_load.at[slot[o]])

    kept = [(own_block, table.at[pl.ds(0, boxes)]), (ops_in, ops_out), (src_in, src_out),
            (tgt_in, tgt_out)]
    kept = [pltpu.make_async_copy(a, b, keep.at[i]) for i, (a, b) in enumerate(kept)]
    for copy in kept:
        copy.start()
    children = {o: [c for c in INTERNAL if PARENT[c] == o] for o in INTERNAL}
    loaded = set()
    for kind, o, arg in PLAN:
        if kind == 0:
            if o == 0:
                if arg == 0:
                    idx_local(0).start()
            else:
                full_copy(o, arg).wait_recv()
            for c in children[o]:
                full_copy(c, arg).start()
            if o == 0 and arg == 1:
                for c in INTERNAL[1:]:
                    idx_copy(c).start()
            if o != 0 and arg == 1:
                idx_copy(o).wait_recv()
                idx_local(o).start()
            continue
        if o not in loaded:
            idx_local(o).wait()
            loaded.add(o)
        block = blocks[o]
        p = pos[arg]

        def pick(g, carry, block=block, p=p):
            for h, stage in ((0, stage_own), (1, stage_other)):
                for i in range(UNROLL):
                    row = block[idx.at[pl.ds(p * pair + h * cap + i, cap)][g * UNROLL]]
                    stage[p, g * UNROLL + i] = row
            return carry

        lax.fori_loop(0, cap // UNROLL, pick, 0)
        owner = torus_add(me_v, o, -1)
        step = torus_step(o, arg) if arg != o else 0
        if arg == o:
            pltpu.make_async_copy(stage_own.at[p], ghost(0, owner), own_local).start()
        else:
            remote(stage_own.at[p], ghost(0, owner), own_send, own_recv, mesh_id(step)).start()
        remote(stage_other.at[p], ghost(1, owner), other_send, other_recv,
               mesh_id(step, 1)).start()

    here = (1 - me_u, me_v)
    inner = len(INTERNAL)
    part = ghost(0, 0, peers - inner)
    side = ghost(1, 0, peers)
    remote(part, part, own_send, own_recv, here).wait_recv()
    remote(side, side, other_send, other_recv, here).wait_recv()
    remote(part, part, own_send, own_recv, here).wait_send()
    remote(side, side, other_send, other_recv, here).wait_send()
    part = ghost(0, 0, inner)
    pltpu.make_async_copy(part, part, own_local).wait()
    for copy in kept:
        copy.wait()
    for c in INTERNAL[1:]:
        idx_copy(c).wait_send()
        for half in range(2):
            full_copy(c, half).wait_send()


def torus_step(a, b):
    step = 0
    for weight in (SIDE * SIDE, SIDE, 1):
        step += (((b // weight) - (a // weight)) % SIDE) * weight
    return step


def exchange(parents, lists, ops, src, tgt):
    _, peers, cap = lists.shape
    boxes, coeffs = parents.shape
    groups, order, pos = list_layout()
    me_v = lax.axis_index("gy")
    dest = jnp.stack([torus_add(me_v, o) for o in order])
    idx = jnp.transpose(lists, (1, 0, 2))[dest].reshape(-1)
    inner = len(INTERNAL)
    dma = pltpu.SemaphoreType.DMA
    vmem = pl.BlockSpec(memory_space=pltpu.VMEM)
    anym = pl.BlockSpec(memory_space=pl.ANY)

    def kern(*refs):
        comm_kernel(peers, *refs)

    return pl.pallas_call(
        kern,
        in_specs=[vmem, vmem, anym, anym, anym],
        out_specs=[vmem] * 4,
        out_shape=[
            pltpu.VMEM((boxes + 2 * peers * cap, 2, coeffs // 2), parents.dtype),
            pltpu.VMEM(ops.shape, ops.dtype),
            pltpu.VMEM(src.shape, src.dtype),
            pltpu.VMEM(tgt.shape, tgt.dtype),
        ],
        scratch_shapes=[pltpu.VMEM((boxes, 2, coeffs // 2), parents.dtype)] * (inner - 1)
        + [
            pltpu.VMEM(idx.shape, jnp.int32),
            pltpu.SMEM((idx.shape[0] + 1024,), jnp.int32),
            pltpu.VMEM((len(order), cap, 2, coeffs // 2), parents.dtype),
            pltpu.VMEM((len(order), cap, 2, coeffs // 2), parents.dtype),
            dma((2 * inner - 2,)),
            dma((2 * inner - 2,)),
            dma((inner - 1,)),
            dma((inner - 1,)),
            dma((inner,)),
            dma, dma, dma, dma, dma,
            dma((4,)),
        ],
        compiler_params=pltpu.CompilerParams(
            collective_id=0, has_side_effects=True, vmem_limit_bytes=20 << 20
        ),
        name="exchange",
    )(idx, parents.reshape(boxes, 2, coeffs // 2), ops, src, tgt)


def m2l_kernel(ops, chunks_per_op, src_ref, count_ref, tgt_ref, tab_ref, op_ref, out_ref,
               x_ref, y_ref, acc_ref, list_ref):
    boxes, coeffs = acc_ref.shape
    stride = src_ref.shape[0] // CHUNK
    empty = ops * chunks_per_op
    acc_ref[...] = jnp.zeros_like(acc_ref)
    y_ref[...] = jnp.zeros_like(y_ref)

    def fill(o, pos):
        n = lax.div(count_ref[o] + (CHUNK - 1), CHUNK)
        for c in range(chunks_per_op):
            list_ref[pos] = o * chunks_per_op + c
            pos = pos + jnp.where(c < n, 1, 0)
        return pos

    for i in range(BATCH):
        list_ref[i] = empty
    total = lax.fori_loop(0, ops, fill, BATCH)
    for i in range(3 * BATCH):
        list_ref[total + i] = empty

    def gather(it):
        for h in range(BATCH):
            ch = list_ref[BATCH * it + h]
            for i in range(CHUNK):
                s = src_ref.at[pl.ds(i * stride, stride)][ch]
                x_ref[h * CHUNK + i] = tab_ref[s].astype(jnp.float32)

    def translate(it):
        x2 = x_ref.reshape(2 * BATCH * CHUNK, x_ref.shape[2])
        for h in range(BATCH):
            ch = list_ref[BATCH * it + h]
            first = 2 * CHUNK * h
            lo = x2[pl.ds(first, CHUNK, stride=2), :].astype(jnp.bfloat16)
            hi = x2[pl.ds(first + 1, CHUNK, stride=2), :].astype(jnp.bfloat16)
            o = jnp.minimum(lax.div(ch, chunks_per_op), ops - 1)
            w = op_ref[pl.ds(pl.multiple_of(o * coeffs, coeffs), coeffs), :]
            y_ref[h * CHUNK : (h + 1) * CHUNK, :] = jnp.dot(
                jnp.concatenate([lo, hi], axis=1), w, preferred_element_type=jnp.float32
            ).astype(jnp.bfloat16)

    def scatter(it):
        rows = lax.broadcasted_iota(jnp.int32, (boxes, CHUNK), 0)
        ps = []
        for h in range(BATCH):
            t = tgt_ref[pl.ds(list_ref[BATCH * it + h], 1), :]
            ps.append(jnp.where(rows == t, 1.0, 0.0).astype(jnp.bfloat16))
        acc_ref[...] += jnp.dot(
            jnp.concatenate(ps, axis=1), y_ref[...], preferred_element_type=jnp.float32
        )

    gather(1)

    @pl.loop(1, lax.div(total + BATCH - 1, BATCH) + 1)
    def _(j):
        scatter(j - 1)
        translate(j)
        gather(j + 1)

    out_ref[...] = acc_ref[...].astype(out_ref.dtype)


def prepare(src, tgt, counts):
    ops, slots = src.shape
    chunks = ops * slots // CHUNK
    position = jnp.arange(slots, dtype=jnp.int32)[None, :]
    tgt = jnp.where(position < counts[:, None], tgt, -1)
    tgt = jnp.pad(tgt.reshape(-1, CHUNK), ((0, 8), (0, 0)), constant_values=-1)
    stride = -(-(chunks + 1) // 128) * 128
    src = jnp.pad(src.reshape(-1, CHUNK).T, ((0, 0), (0, stride - chunks))).reshape(-1)
    return src, tgt


def m2l(table, src, tgt, counts, m2l_ops, slots, boxes):
    ops = counts.shape[0]
    coeffs = m2l_ops.shape[1]
    chunks_per_op = slots // CHUNK
    chunks = ops * chunks_per_op
    smem = pl.BlockSpec(memory_space=pltpu.SMEM)
    vmem = pl.BlockSpec(memory_space=pltpu.VMEM)

    def kern(*refs):
        m2l_kernel(ops, chunks_per_op, *refs)

    return pl.pallas_call(
        kern,
        in_specs=[smem, smem, vmem, vmem, vmem],
        out_specs=vmem,
        out_shape=jax.ShapeDtypeStruct((boxes, coeffs), jnp.bfloat16),
        scratch_shapes=[
            pltpu.VMEM((BATCH * CHUNK, 2, coeffs // 2), jnp.float32),
            pltpu.VMEM((BATCH * CHUNK, coeffs), jnp.bfloat16),
            pltpu.VMEM((boxes, coeffs), jnp.float32),
            pltpu.SMEM((chunks + 4 * BATCH,), jnp.int32),
        ],
        compiler_params=pltpu.CompilerParams(vmem_limit_bytes=8 << 20),
        name="m2l",
    )(
        src,
        counts,
        pltpu.with_memory_space_constraint(tgt, pltpu.VMEM),
        pltpu.with_memory_space_constraint(table, pltpu.VMEM),
        pltpu.with_memory_space_constraint(m2l_ops, pltpu.VMEM),
    )


def body(
    leaf_multipoles, m2m_ops, m2l_ops, l2l_ops, send_boxes, task_source, task_target, task_count
):
    coeff_count = leaf_multipoles.shape[1]
    box_count = leaf_multipoles.shape[0] // 8
    column = lax.axis_index("gx")
    leaves = leaf_multipoles.reshape(box_count, 8, coeff_count)
    parents = jnp.einsum("bcp,cpq->bq", leaves, m2m_ops, preferred_element_type=jnp.float32).astype(
        jnp.bfloat16
    )
    boxes = send_boxes[0]
    cap = boxes.shape[-1]
    peers = boxes.shape[1]
    other = jnp.where(column == 0, boxes[2], boxes[0])
    lists = jnp.stack([boxes[1], other], 0)
    sources = task_source[0]
    block = peers * cap
    rows = box_count + 2 * block
    own = jnp.logical_and(sources >= box_count, sources < box_count + block)
    shifted = jnp.where(
        jnp.logical_and(column == 1, own), sources + block, sources - block
    )
    src = jnp.where(sources < box_count, sources, shifted)
    src = jnp.clip(src, 0, rows - 1)
    src, tgt = prepare(src, task_target[0], task_count[0])
    ops = m2l_ops.reshape(-1, coeff_count)
    table, ops, src, tgt = exchange(parents, lists, ops, src, tgt)
    slots = task_target.shape[2]
    parent_rounded = m2l(table, src, tgt, task_count[0], ops, slots, box_count)
    leaf_local = jnp.einsum(
        "bp,cpq->bcq", parent_rounded, l2l_ops, preferred_element_type=jnp.float32
    )
    return leaf_local.reshape(-1, coeff_count)


def solution(mesh):
    return jax.shard_map(
        body,
        mesh=mesh,
        in_specs=(
            P(("gx", "gy"), None),
            P(),
            P(),
            P(),
            P(("gx", "gy"), None, None, None),
            P(("gx", "gy"), None, None),
            P(("gx", "gy"), None, None),
            P(("gx", "gy"), None),
        ),
        out_specs=P(("gx", "gy"), None),
        check_vma=False,
    )
```

```python
import jax
import jax.numpy as jnp
from jax import lax
from jax.experimental import pallas as pl
from jax.experimental.pallas import tpu as pltpu
from jax.sharding import PartitionSpec as P

CHUNK = 128
BATCH = 4
SIDE = 4
UNROLL = 32

INTERNAL = (0, 12, 4, 48, 28, 7, 49, 52, 29, 11, 6, 23, 45, 10, 22, 41, 46, 47)
PARENT = (-1, 0, 6, 7, 0, 6, 7, 4, 12, 10, 6, 7, 0, 29, 10, 12, 0, 29, 22, 23, 4, 22, 23, 7, 28, 41, 22, 11, 12, 28, 29, 47, 48, 49, 46, 47, 52, 41, 22, 23, 41, 45, 41, 47, 45, 29, 45, 46, 0, 48, 49, 48, 48, 52, 6, 7, 52, 41, 10, 11, 12, 49, 46, 47)
PLAN = (
    (0, 0, 0), (0, 0, 1), (1, 0, 0), (1, 0, 1), (1, 0, 16), (0, 12, 0), (0, 4, 0), (0, 48, 0),
    (0, 12, 1), (0, 4, 1), (0, 48, 1), (1, 12, 12), (1, 12, 8), (1, 12, 15), (1, 12, 60),
    (1, 4, 4), (1, 4, 20), (0, 28, 0), (0, 7, 0), (0, 49, 0), (1, 48, 48), (1, 48, 32),
    (1, 48, 51), (0, 52, 0), (0, 28, 1), (0, 7, 1), (0, 49, 1), (1, 28, 28), (1, 28, 24),
    (1, 7, 7), (1, 7, 3), (1, 7, 55), (0, 52, 1), (1, 49, 49), (1, 49, 33), (1, 49, 50),
    (1, 49, 61), (1, 52, 52), (1, 52, 36), (0, 29, 0), (1, 52, 53), (1, 52, 56), (0, 11, 0),
    (0, 29, 1), (0, 6, 0), (0, 23, 0), (1, 29, 29), (1, 29, 13), (1, 29, 17), (1, 29, 30),
    (0, 11, 1), (1, 11, 11), (1, 11, 27), (1, 11, 59), (0, 23, 1), (1, 23, 23), (1, 23, 19),
    (1, 23, 39), (0, 45, 0), (0, 6, 1), (1, 6, 6), (1, 6, 2), (1, 6, 5), (1, 6, 54), (0, 10, 0),
    (0, 45, 1), (0, 22, 0), (1, 45, 45), (1, 45, 44), (0, 41, 0), (0, 46, 0), (0, 22, 1),
    (1, 22, 22), (1, 22, 18), (1, 22, 21), (1, 22, 26), (1, 22, 38), (0, 10, 1), (1, 10, 10),
    (1, 10, 9), (1, 10, 14), (1, 10, 58), (0, 46, 1), (1, 46, 46), (1, 46, 34), (1, 46, 62),
    (0, 41, 1), (1, 41, 41), (1, 41, 25), (1, 41, 37), (0, 47, 0), (1, 41, 40), (1, 41, 42),
    (1, 41, 57), (0, 47, 1), (1, 47, 47), (1, 47, 31), (1, 47, 35), (1, 47, 43), (1, 47, 63),
)

PAD = 4


def list_layout():
    groups, order, pos = {}, [], {}
    for o in INTERNAL:
        members = [o] + [c for c in range(len(PARENT)) if PARENT[c] == o and c not in INTERNAL]
        start = len(order)
        for c in members:
            pos[c] = len(order)
            order.append(c)
        while len(order) % PAD:
            order.append(o)
        groups[o] = (start, len(order) - start)
    return groups, order, pos


def torus_add(base, offset, sign=1):
    parts = []
    for weight in (SIDE * SIDE, SIDE, 1):
        a = lax.rem(lax.div(base, weight), SIDE)
        b = (offset // weight) % SIDE
        if sign < 0:
            b = (SIDE - b) % SIDE
        parts.append(lax.rem(a + b, SIDE) * weight)
    return parts[0] + parts[1] + parts[2]


def comm_kernel(peers, idx_in, own_block, ops_in, src_in, tgt_in, table, ops_out, src_out, tgt_out, *scratch):
    blocks = dict(zip(INTERNAL, (own_block,) + scratch[: len(INTERNAL) - 1]))
    scratch = scratch[len(INTERNAL) - 1 :]
    (land, idx, stage_own, stage_other, full_send, full_recv, idx_send, idx_recv, idx_load,
     own_send, own_recv, own_local, other_send, other_recv, keep) = scratch
    groups, order, pos = list_layout()
    slot = {o: i for i, o in enumerate(INTERNAL)}
    cap = stage_own.shape[1]
    boxes = own_block.shape[0]
    half_rows = own_block.shape[0] // 2
    pair = 2 * cap
    me_u = lax.axis_index("gx")
    me_v = lax.axis_index("gy")
    ready = pltpu.get_barrier_semaphore()

    def mesh_id(offset, side=0, sign=1):
        column = me_u if side == 0 else 1 - me_u
        return (column, torus_add(me_v, offset, sign))

    near = [s * w for w in (SIDE * SIDE, SIDE, 1) for s in (1, SIDE - 1)]
    sends = [(o, 0) for o in sorted(set(near) | set(INTERNAL[1:]))]
    sends += [(o, 1) for o in [0] + near]
    for o, side in sends:
        pl.semaphore_signal(ready, inc=1, device_id=mesh_id(o, side, -1),
                            device_id_type=pl.DeviceIdType.MESH)
    pl.semaphore_wait(ready, len(sends))

    def ghost(side, owner, count=1):
        first = boxes + (side * peers + owner) * cap
        return table.at[pl.ds(first, count * cap)]

    def remote(src, dst, send, recv, target):
        return pltpu.make_async_remote_copy(
            src_ref=src, dst_ref=dst, send_sem=send, recv_sem=recv, device_id=target,
            device_id_type=pl.DeviceIdType.MESH,
        )

    def full_copy(child, half):
        parent = PARENT[child]
        rows = pl.ds(half * half_rows, half_rows)
        step = torus_step(parent, child)
        k = (slot[child] - 1) * 2 + half
        return remote(blocks[parent].at[rows], blocks[child].at[rows], full_send.at[k],
                      full_recv.at[k], mesh_id(step))

    def idx_copy(o):
        start, n = groups[o]
        part = pl.ds(start * pair, n * pair)
        return remote(idx_in.at[part], land.at[part], idx_send, idx_recv, mesh_id(o))

    mine = pl.ds(0, groups[0][1] * pair)
    rest = pl.ds(groups[0][1] * pair, (len(order) - groups[0][1]) * pair)
    load_mine = pltpu.make_async_copy(idx_in.at[mine], idx.at[mine], idx_load.at[0])
    load_rest = pltpu.make_async_copy(land.at[rest], idx.at[rest], idx_load.at[1])
    load_mine.start()
    for c in INTERNAL[1:]:
        idx_copy(c).start()
    kept = [(own_block, table.at[pl.ds(0, boxes)]), (ops_in, ops_out), (src_in, src_out),
            (tgt_in, tgt_out)]
    kept = [pltpu.make_async_copy(a, b, keep.at[i]) for i, (a, b) in enumerate(kept)]
    for copy in kept:
        copy.start()
    here = (1 - me_u, me_v)
    children = {o: [c for c in INTERNAL if PARENT[c] == o] for o in INTERNAL}
    loaded = set()
    for kind, o, arg in PLAN:
        if kind == 0:
            if o != 0:
                if 0 in loaded and 1 not in loaded:
                    remote(idx_in.at[rest], land.at[rest], idx_send, idx_recv, here).wait_recv()
                    load_rest.start()
                    loaded.add(1)
                full_copy(o, arg).wait_recv()
            for c in children[o]:
                full_copy(c, arg).start()
            continue
        if o == 0 and 0 not in loaded:
            load_mine.wait()
            loaded.add(0)
        if o != 0 and 2 not in loaded:
            load_rest.wait()
            loaded.add(2)
        block = blocks[o]
        p = pos[arg]

        def pick(g, carry, block=block, p=p):
            for h, stage in ((0, stage_own), (1, stage_other)):
                for i in range(UNROLL):
                    row = block[idx.at[pl.ds(p * pair + h * cap + i, cap)][g * UNROLL]]
                    stage[p, g * UNROLL + i] = row
            return carry

        lax.fori_loop(0, cap // UNROLL, pick, 0)
        owner = torus_add(me_v, o, -1)
        step = torus_step(o, arg) if arg != o else 0
        if arg == o:
            pltpu.make_async_copy(stage_own.at[p], ghost(0, owner), own_local).start()
        else:
            remote(stage_own.at[p], ghost(0, owner), own_send, own_recv, mesh_id(step)).start()
        remote(stage_other.at[p], ghost(1, owner), other_send, other_recv,
               mesh_id(step, 1)).start()

    inner = len(INTERNAL)
    part = ghost(0, 0, peers - inner)
    side = ghost(1, 0, peers)
    remote(part, part, own_send, own_recv, here).wait_recv()
    remote(side, side, other_send, other_recv, here).wait_recv()
    remote(part, part, own_send, own_recv, here).wait_send()
    remote(side, side, other_send, other_recv, here).wait_send()
    part = ghost(0, 0, inner)
    pltpu.make_async_copy(part, part, own_local).wait()
    for copy in kept:
        copy.wait()
    remote(idx_in.at[rest], land.at[rest], idx_send, idx_recv, here).wait_send()
    for c in INTERNAL[1:]:
        for half in range(2):
            full_copy(c, half).wait_send()


def torus_step(a, b):
    step = 0
    for weight in (SIDE * SIDE, SIDE, 1):
        step += (((b // weight) - (a // weight)) % SIDE) * weight
    return step


def exchange(parents, lists, ops, src, tgt):
    _, peers, cap = lists.shape
    boxes, coeffs = parents.shape
    groups, order, pos = list_layout()
    me_v = lax.axis_index("gy")
    dest = jnp.stack([torus_add(me_v, o) for o in order])
    idx = jnp.transpose(lists, (1, 0, 2))[dest].reshape(-1)
    inner = len(INTERNAL)
    dma = pltpu.SemaphoreType.DMA
    vmem = pl.BlockSpec(memory_space=pltpu.VMEM)
    anym = pl.BlockSpec(memory_space=pl.ANY)

    def kern(*refs):
        comm_kernel(peers, *refs)

    return pl.pallas_call(
        kern,
        in_specs=[vmem, vmem, anym, anym, anym],
        out_specs=[vmem] * 4,
        out_shape=[
            pltpu.VMEM((boxes + 2 * peers * cap, 2, coeffs // 2), parents.dtype),
            pltpu.VMEM(ops.shape, ops.dtype),
            pltpu.VMEM(src.shape, src.dtype),
            pltpu.VMEM(tgt.shape, tgt.dtype),
        ],
        scratch_shapes=[pltpu.VMEM((boxes, 2, coeffs // 2), parents.dtype)] * (inner - 1)
        + [
            pltpu.VMEM(idx.shape, jnp.int32),
            pltpu.SMEM((idx.shape[0] + 1024,), jnp.int32),
            pltpu.VMEM((len(order), cap, 2, coeffs // 2), parents.dtype),
            pltpu.VMEM((len(order), cap, 2, coeffs // 2), parents.dtype),
            dma((2 * inner - 2,)),
            dma((2 * inner - 2,)),
            dma,
            dma,
            dma((2,)),
            dma, dma, dma, dma, dma,
            dma((4,)),
        ],
        compiler_params=pltpu.CompilerParams(
            collective_id=0, has_side_effects=True, vmem_limit_bytes=20 << 20
        ),
        name="exchange",
    )(idx, parents.reshape(boxes, 2, coeffs // 2),
      *(pltpu.with_memory_space_constraint(a, pltpu.HBM) for a in (ops, src, tgt)))


def m2l_kernel(ops, chunks_per_op, src_ref, count_ref, tgt_ref, tab_ref, op_ref, out_ref,
               x_ref, y_ref, acc_ref, list_ref):
    boxes, coeffs = acc_ref.shape
    size = src_ref.shape[0]
    empty = size
    acc_ref[...] = jnp.zeros_like(acc_ref)
    y_ref[...] = jnp.zeros_like(y_ref)

    def fill(o, pos):
        n = lax.div(count_ref[o] + (CHUNK - 1), CHUNK)
        first = lax.div(o, 8) * (8 * CHUNK * chunks_per_op) + lax.rem(o, 8) * CHUNK
        for c in range(chunks_per_op):
            list_ref[pos] = first + c * (8 * CHUNK)
            pos = pos + jnp.where(c < n, 1, 0)
        return pos

    def locate(first):
        o = lax.div(first, 8 * CHUNK * chunks_per_op) * 8 + lax.rem(lax.div(first, CHUNK), 8)
        c = lax.rem(lax.div(first, 8 * CHUNK), chunks_per_op)
        return jnp.minimum(o, ops - 1), c

    for i in range(BATCH):
        list_ref[i] = empty
    total = lax.fori_loop(0, ops, fill, BATCH)
    for i in range(3 * BATCH):
        list_ref[total + i] = empty

    def gather(it):
        for h in range(BATCH):
            first = list_ref[BATCH * it + h]
            first = jnp.where(first < empty, first, 0)
            for i in range(CHUNK):
                s = src_ref.at[pl.ds(i, size - CHUNK + 1)][first]
                x_ref[h * CHUNK + i] = tab_ref[s].astype(jnp.float32)

    def translate(it):
        x2 = x_ref.reshape(2 * BATCH * CHUNK, x_ref.shape[2])
        for h in range(BATCH):
            o, _ = locate(list_ref[BATCH * it + h])
            first = 2 * CHUNK * h
            lo = x2[pl.ds(first, CHUNK, stride=2), :].astype(jnp.bfloat16)
            hi = x2[pl.ds(first + 1, CHUNK, stride=2), :].astype(jnp.bfloat16)
            w = op_ref[pl.ds(pl.multiple_of(o * coeffs, coeffs), coeffs), :]
            y_ref[h * CHUNK : (h + 1) * CHUNK, :] = jnp.dot(
                jnp.concatenate([lo, hi], axis=1), w, preferred_element_type=jnp.float32
            ).astype(jnp.bfloat16)

    def scatter(it):
        rows = lax.broadcasted_iota(jnp.int32, (boxes, CHUNK), 0)
        ps = []
        for h in range(BATCH):
            first = list_ref[BATCH * it + h]
            o, c = locate(first)
            used = jnp.where(first < empty, count_ref[o] - c * CHUNK, 0)
            first = jnp.where(first < empty, first, 0)
            t = tgt_ref[pl.ds(lax.div(first, CHUNK), 1), :]
            t = jnp.where(lax.broadcasted_iota(jnp.int32, (1, CHUNK), 1) < used, t, -1)
            ps.append(jnp.where(rows == t, 1.0, 0.0).astype(jnp.bfloat16))
        acc_ref[...] += jnp.dot(
            jnp.concatenate(ps, axis=1), y_ref[...], preferred_element_type=jnp.float32
        )

    gather(1)

    @pl.loop(1, lax.div(total + BATCH - 1, BATCH) + 1)
    def _(j):
        scatter(j - 1)
        translate(j)
        gather(j + 1)

    out_ref[...] = acc_ref[...].astype(out_ref.dtype)


def m2l(table, src, tgt, counts, m2l_ops, slots, boxes):
    ops = counts.shape[0]
    coeffs = m2l_ops.shape[1]
    chunks_per_op = slots // CHUNK
    chunks = ops * chunks_per_op
    smem = pl.BlockSpec(memory_space=pltpu.SMEM)
    vmem = pl.BlockSpec(memory_space=pltpu.VMEM)

    def kern(*refs):
        m2l_kernel(ops, chunks_per_op, *refs)

    return pl.pallas_call(
        kern,
        in_specs=[smem, smem, vmem, vmem, vmem],
        out_specs=vmem,
        out_shape=jax.ShapeDtypeStruct((boxes, coeffs), jnp.bfloat16),
        scratch_shapes=[
            pltpu.VMEM((BATCH * CHUNK, 2, coeffs // 2), jnp.float32),
            pltpu.VMEM((BATCH * CHUNK, coeffs), jnp.bfloat16),
            pltpu.VMEM((boxes, coeffs), jnp.float32),
            pltpu.SMEM((chunks + 4 * BATCH,), jnp.int32),
        ],
        compiler_params=pltpu.CompilerParams(vmem_limit_bytes=8 << 20),
        name="m2l",
    )(
        src,
        counts,
        pltpu.with_memory_space_constraint(tgt, pltpu.VMEM),
        pltpu.with_memory_space_constraint(table, pltpu.VMEM),
        pltpu.with_memory_space_constraint(m2l_ops, pltpu.VMEM),
    )


def body(
    leaf_multipoles, m2m_ops, m2l_ops, l2l_ops, send_boxes, task_source, task_target, task_count
):
    coeff_count = leaf_multipoles.shape[1]
    box_count = leaf_multipoles.shape[0] // 8
    column = lax.axis_index("gx")
    leaves = leaf_multipoles.reshape(box_count, 8, coeff_count)
    parents = jnp.einsum("bcp,cpq->bq", leaves, m2m_ops, preferred_element_type=jnp.float32).astype(
        jnp.bfloat16
    )
    boxes = send_boxes[0]
    cap = boxes.shape[-1]
    peers = boxes.shape[1]
    other = jnp.where(column == 0, boxes[2], boxes[0])
    lists = jnp.stack([boxes[1], other], 0)
    sources = task_source[0]
    block = peers * cap
    rows = box_count + 2 * block
    own = jnp.logical_and(sources >= box_count, sources < box_count + block)
    shifted = jnp.where(
        jnp.logical_and(column == 1, own), sources + block, sources - block
    )
    src = jnp.where(sources < box_count, sources, shifted)
    src = jnp.clip(src, 0, rows - 1)
    slots = src.shape[1]
    src, tgt = (
        a.reshape(-1, 8, slots // CHUNK, CHUNK).transpose(0, 2, 1, 3).reshape(-1, CHUNK)
        for a in (src, task_target[0])
    )
    src = src.reshape(-1)
    ops = m2l_ops.reshape(-1, coeff_count)
    table, ops, src, tgt = exchange(parents, lists, ops, src, tgt)
    parent_rounded = m2l(table, src, tgt, task_count[0], ops, slots, box_count)
    leaf_local = jnp.einsum(
        "bp,cpq->bcq", parent_rounded, l2l_ops, preferred_element_type=jnp.float32
    )
    return leaf_local.reshape(-1, coeff_count)


def solution(mesh):
    return jax.shard_map(
        body,
        mesh=mesh,
        in_specs=(
            P(("gx", "gy"), None),
            P(),
            P(),
            P(),
            P(("gx", "gy"), None, None, None),
            P(("gx", "gy"), None, None),
            P(("gx", "gy"), None, None),
            P(("gx", "gy"), None),
        ),
        out_specs=P(("gx", "gy"), None),
        check_vma=False,
    )
```

```python
import jax
import jax.numpy as jnp
from jax import lax
from jax.experimental import pallas as pl
from jax.experimental.pallas import tpu as pltpu
from jax.sharding import PartitionSpec as P

CHUNK = 128
BATCH = 4
SIDE = 4
UNROLL = 32

INTERNAL = (0, 12, 4, 48, 28, 7, 49, 52, 29, 11, 6, 23, 45, 10, 22, 41, 46, 47)
PARENT = (-1, 0, 6, 7, 0, 6, 7, 4, 12, 10, 6, 7, 0, 29, 10, 12, 0, 29, 22, 23, 4, 22, 23, 7, 28, 41, 22, 11, 12, 28, 29, 47, 48, 49, 46, 47, 52, 41, 22, 23, 41, 45, 41, 47, 45, 29, 45, 46, 0, 48, 49, 48, 48, 52, 6, 7, 52, 41, 10, 11, 12, 49, 46, 47)
PLAN = (
    (0, 0, 0), (0, 0, 1), (1, 0, 0), (1, 0, 1), (1, 0, 16), (0, 12, 0), (0, 4, 0), (0, 48, 0),
    (0, 12, 1), (0, 4, 1), (0, 48, 1), (1, 12, 12), (1, 12, 8), (1, 12, 15), (1, 12, 60),
    (1, 4, 4), (1, 4, 20), (0, 28, 0), (0, 7, 0), (0, 49, 0), (1, 48, 48), (1, 48, 32),
    (1, 48, 51), (0, 52, 0), (0, 28, 1), (0, 7, 1), (0, 49, 1), (1, 28, 28), (1, 28, 24),
    (1, 7, 7), (1, 7, 3), (1, 7, 55), (0, 52, 1), (1, 49, 49), (1, 49, 33), (1, 49, 50),
    (1, 49, 61), (1, 52, 52), (1, 52, 36), (0, 29, 0), (1, 52, 53), (1, 52, 56), (0, 11, 0),
    (0, 29, 1), (0, 6, 0), (0, 23, 0), (1, 29, 29), (1, 29, 13), (1, 29, 17), (1, 29, 30),
    (0, 11, 1), (1, 11, 11), (1, 11, 27), (1, 11, 59), (0, 23, 1), (1, 23, 23), (1, 23, 19),
    (1, 23, 39), (0, 45, 0), (0, 6, 1), (1, 6, 6), (1, 6, 2), (1, 6, 5), (1, 6, 54), (0, 10, 0),
    (0, 45, 1), (0, 22, 0), (1, 45, 45), (1, 45, 44), (0, 41, 0), (0, 46, 0), (0, 22, 1),
    (1, 22, 22), (1, 22, 18), (1, 22, 21), (1, 22, 26), (1, 22, 38), (0, 10, 1), (1, 10, 10),
    (1, 10, 9), (1, 10, 14), (1, 10, 58), (0, 46, 1), (1, 46, 46), (1, 46, 34), (1, 46, 62),
    (0, 41, 1), (1, 41, 41), (1, 41, 25), (1, 41, 37), (0, 47, 0), (1, 41, 40), (1, 41, 42),
    (1, 41, 57), (0, 47, 1), (1, 47, 47), (1, 47, 31), (1, 47, 35), (1, 47, 43), (1, 47, 63),
)

PAD = 4


def list_layout():
    groups, order, pos = {}, [], {}
    for o in INTERNAL:
        members = [o] + [c for c in range(len(PARENT)) if PARENT[c] == o and c not in INTERNAL]
        start = len(order)
        for c in members:
            pos[c] = len(order)
            order.append(c)
        while len(order) % PAD:
            order.append(o)
        groups[o] = (start, len(order) - start)
    return groups, order, pos


def torus_add(base, offset, sign=1):
    parts = []
    for weight in (SIDE * SIDE, SIDE, 1):
        a = lax.rem(lax.div(base, weight), SIDE)
        b = (offset // weight) % SIDE
        if sign < 0:
            b = (SIDE - b) % SIDE
        parts.append(lax.rem(a + b, SIDE) * weight)
    return parts[0] + parts[1] + parts[2]


def comm_kernel(peers, idx_in, own_block, ops_in, src_in, tgt_in, l2l_in, table,
                ops_out, src_out, tgt_out, l2l_out, *scratch):
    blocks = dict(zip(INTERNAL, (own_block,) + scratch[: len(INTERNAL) - 1]))
    scratch = scratch[len(INTERNAL) - 1 :]
    (land, idx, stage_own, stage_other, full_send, full_recv, idx_send, idx_recv, idx_load,
     own_send, own_recv, own_local, other_send, other_recv, keep) = scratch
    groups, order, pos = list_layout()
    slot = {o: i for i, o in enumerate(INTERNAL)}
    cap = stage_own.shape[1]
    boxes = own_block.shape[0]
    half_rows = own_block.shape[0] // 2
    pair = 2 * cap
    me_u = lax.axis_index("gx")
    me_v = lax.axis_index("gy")
    ready = pltpu.get_barrier_semaphore()

    def mesh_id(offset, side=0, sign=1):
        column = me_u if side == 0 else 1 - me_u
        return (column, torus_add(me_v, offset, sign))

    near = [s * w for w in (SIDE * SIDE, SIDE, 1) for s in (1, SIDE - 1)]
    sends = [(o, 0) for o in sorted(set(near) | set(INTERNAL[1:]))]
    sends += [(o, 1) for o in [0] + near]
    for o, side in sends:
        pl.semaphore_signal(ready, inc=1, device_id=mesh_id(o, side, -1),
                            device_id_type=pl.DeviceIdType.MESH)
    pl.semaphore_wait(ready, len(sends))

    def ghost(side, owner, count=1):
        first = boxes + (side * peers + owner) * cap
        return table.at[pl.ds(first, count * cap)]

    def remote(src, dst, send, recv, target):
        return pltpu.make_async_remote_copy(
            src_ref=src, dst_ref=dst, send_sem=send, recv_sem=recv, device_id=target,
            device_id_type=pl.DeviceIdType.MESH,
        )

    def full_copy(child, half):
        parent = PARENT[child]
        rows = pl.ds(half * half_rows, half_rows)
        step = torus_step(parent, child)
        k = (slot[child] - 1) * 2 + half
        return remote(blocks[parent].at[rows], blocks[child].at[rows], full_send.at[k],
                      full_recv.at[k], mesh_id(step))

    def idx_copy(o):
        start, n = groups[o]
        part = pl.ds(start * pair, n * pair)
        return remote(idx_in.at[part], land.at[part], idx_send, idx_recv, mesh_id(o))

    mine = pl.ds(0, groups[0][1] * pair)
    rest = pl.ds(groups[0][1] * pair, (len(order) - groups[0][1]) * pair)
    load_mine = pltpu.make_async_copy(idx_in.at[mine], idx.at[mine], idx_load.at[0])
    load_rest = pltpu.make_async_copy(land.at[rest], idx.at[rest], idx_load.at[1])
    load_mine.start()
    for c in INTERNAL[1:]:
        idx_copy(c).start()
    kept = [(own_block, table.at[pl.ds(0, boxes)]), (ops_in, ops_out), (src_in, src_out),
            (tgt_in, tgt_out), (l2l_in, l2l_out)]
    kept = [pltpu.make_async_copy(a, b, keep.at[i]) for i, (a, b) in enumerate(kept)]
    for copy in kept:
        copy.start()
    here = (1 - me_u, me_v)
    children = {o: [c for c in INTERNAL if PARENT[c] == o] for o in INTERNAL}
    loaded = set()
    for kind, o, arg in PLAN:
        if kind == 0:
            if o != 0:
                if 0 in loaded and 1 not in loaded:
                    remote(idx_in.at[rest], land.at[rest], idx_send, idx_recv, here).wait_recv()
                    load_rest.start()
                    loaded.add(1)
                full_copy(o, arg).wait_recv()
            for c in children[o]:
                full_copy(c, arg).start()
            continue
        if o == 0 and 0 not in loaded:
            load_mine.wait()
            loaded.add(0)
        if o != 0 and 2 not in loaded:
            load_rest.wait()
            loaded.add(2)
        block = blocks[o]
        p = pos[arg]

        def pick(g, carry, block=block, p=p):
            for h, stage in ((0, stage_own), (1, stage_other)):
                for i in range(UNROLL):
                    row = block[idx.at[pl.ds(p * pair + h * cap + i, cap)][g * UNROLL]]
                    stage[p, g * UNROLL + i] = row
            return carry

        lax.fori_loop(0, cap // UNROLL, pick, 0)
        owner = torus_add(me_v, o, -1)
        step = torus_step(o, arg) if arg != o else 0
        if arg == o:
            pltpu.make_async_copy(stage_own.at[p], ghost(0, owner), own_local).start()
        else:
            remote(stage_own.at[p], ghost(0, owner), own_send, own_recv, mesh_id(step)).start()
        remote(stage_other.at[p], ghost(1, owner), other_send, other_recv,
               mesh_id(step, 1)).start()

    inner = len(INTERNAL)
    part = ghost(0, 0, peers - inner)
    side = ghost(1, 0, peers)
    remote(part, part, own_send, own_recv, here).wait_recv()
    remote(side, side, other_send, other_recv, here).wait_recv()
    remote(part, part, own_send, own_recv, here).wait_send()
    remote(side, side, other_send, other_recv, here).wait_send()
    part = ghost(0, 0, inner)
    pltpu.make_async_copy(part, part, own_local).wait()
    for copy in kept:
        copy.wait()
    block = peers * cap
    rows = src_out[...]
    first = jnp.logical_and(rows >= boxes, rows < boxes + block)
    moved = jnp.where(jnp.logical_and(me_u == 1, first), rows + block, rows - block)
    rows = jnp.where(rows < boxes, rows, moved)
    src_out[...] = jnp.clip(rows, 0, boxes + 2 * block - 1)
    remote(idx_in.at[rest], land.at[rest], idx_send, idx_recv, here).wait_send()
    for c in INTERNAL[1:]:
        for half in range(2):
            full_copy(c, half).wait_send()


def torus_step(a, b):
    step = 0
    for weight in (SIDE * SIDE, SIDE, 1):
        step += (((b // weight) - (a // weight)) % SIDE) * weight
    return step


def exchange(parents, lists, ops, src, tgt, l2l):
    _, peers, cap = lists.shape
    boxes, coeffs = parents.shape
    groups, order, pos = list_layout()
    me_v = lax.axis_index("gy")
    dest = jnp.stack([torus_add(me_v, o) for o in order])
    idx = jnp.transpose(lists, (1, 0, 2))[dest].reshape(-1)
    inner = len(INTERNAL)
    dma = pltpu.SemaphoreType.DMA
    vmem = pl.BlockSpec(memory_space=pltpu.VMEM)
    anym = pl.BlockSpec(memory_space=pl.ANY)

    def kern(*refs):
        comm_kernel(peers, *refs)

    return pl.pallas_call(
        kern,
        in_specs=[vmem, vmem, anym, anym, anym, anym],
        out_specs=[vmem] * 5,
        out_shape=[
            pltpu.VMEM((boxes + 2 * peers * cap, 2, coeffs // 2), parents.dtype),
            pltpu.VMEM(ops.shape, ops.dtype),
            pltpu.VMEM(src.shape, src.dtype),
            pltpu.VMEM(tgt.shape, tgt.dtype),
            pltpu.VMEM(l2l.shape, l2l.dtype),
        ],
        scratch_shapes=[pltpu.VMEM((boxes, 2, coeffs // 2), parents.dtype)] * (inner - 1)
        + [
            pltpu.VMEM(idx.shape, jnp.int32),
            pltpu.SMEM((idx.shape[0] + 1024,), jnp.int32),
            pltpu.VMEM((len(order), cap, 2, coeffs // 2), parents.dtype),
            pltpu.VMEM((len(order), cap, 2, coeffs // 2), parents.dtype),
            dma((2 * inner - 2,)),
            dma((2 * inner - 2,)),
            dma,
            dma,
            dma((2,)),
            dma, dma, dma, dma, dma,
            dma((5,)),
        ],
        compiler_params=pltpu.CompilerParams(
            collective_id=0, has_side_effects=True, vmem_limit_bytes=20 << 20
        ),
        name="exchange",
    )(idx, parents.reshape(boxes, 2, coeffs // 2),
      *(pltpu.with_memory_space_constraint(a, pltpu.HBM) for a in (ops, src, tgt, l2l)))


def m2l_kernel(ops, chunks_per_op, src_ref, count_ref, tgt_ref, tab_ref, op_ref, l2l_ref, out_hbm,
               x_ref, y_ref, acc_ref, list_ref, leaf_ref, sem):
    boxes, coeffs = acc_ref.shape
    size = src_ref.shape[0]
    empty = size
    acc_ref[...] = jnp.zeros_like(acc_ref)
    y_ref[...] = jnp.zeros_like(y_ref)

    def fill(o, pos):
        n = lax.div(count_ref[o] + (CHUNK - 1), CHUNK)
        first = lax.div(o, 8) * (8 * CHUNK * chunks_per_op) + lax.rem(o, 8) * CHUNK
        for c in range(chunks_per_op):
            list_ref[pos] = first + c * (8 * CHUNK)
            pos = pos + jnp.where(c < n, 1, 0)
        return pos

    def locate(first):
        o = lax.div(first, 8 * CHUNK * chunks_per_op) * 8 + lax.rem(lax.div(first, CHUNK), 8)
        c = lax.rem(lax.div(first, 8 * CHUNK), chunks_per_op)
        return jnp.minimum(o, ops - 1), c

    for i in range(BATCH):
        list_ref[i] = empty
    total = lax.fori_loop(0, ops, fill, BATCH)
    for i in range(3 * BATCH):
        list_ref[total + i] = empty

    def gather(it):
        for h in range(BATCH):
            first = list_ref[BATCH * it + h]
            first = jnp.where(first < empty, first, 0)
            for i in range(CHUNK):
                s = src_ref.at[pl.ds(i, size - CHUNK + 1)][first]
                x_ref[h * CHUNK + i] = tab_ref[s].astype(jnp.float32)

    def translate(it):
        x2 = x_ref.reshape(2 * BATCH * CHUNK, x_ref.shape[2])
        for h in range(BATCH):
            o, _ = locate(list_ref[BATCH * it + h])
            first = 2 * CHUNK * h
            lo = x2[pl.ds(first, CHUNK, stride=2), :].astype(jnp.bfloat16)
            hi = x2[pl.ds(first + 1, CHUNK, stride=2), :].astype(jnp.bfloat16)
            w = op_ref[pl.ds(pl.multiple_of(o * coeffs, coeffs), coeffs), :]
            y_ref[h * CHUNK : (h + 1) * CHUNK, :] = jnp.dot(
                jnp.concatenate([lo, hi], axis=1), w, preferred_element_type=jnp.float32
            ).astype(jnp.bfloat16)

    def scatter(it):
        rows = lax.broadcasted_iota(jnp.int32, (boxes, CHUNK), 0)
        ps = []
        for h in range(BATCH):
            first = list_ref[BATCH * it + h]
            o, c = locate(first)
            used = jnp.where(first < empty, count_ref[o] - c * CHUNK, 0)
            first = jnp.where(first < empty, first, 0)
            t = tgt_ref[pl.ds(lax.div(first, CHUNK), 1), :]
            t = jnp.where(lax.broadcasted_iota(jnp.int32, (1, CHUNK), 1) < used, t, -1)
            ps.append(jnp.where(rows == t, 1.0, 0.0).astype(jnp.bfloat16))
        acc_ref[...] += jnp.dot(
            jnp.concatenate(ps, axis=1), y_ref[...], preferred_element_type=jnp.float32
        )

    gather(1)

    @pl.loop(1, lax.div(total + BATCH - 1, BATCH) + 1)
    def _(j):
        scatter(j - 1)
        translate(j)
        gather(j + 1)

    half = boxes // 2
    octants = l2l_ref.shape[0] // coeffs
    span = half * octants
    lanes = leaf_ref.shape[2]
    sends = []
    for k in range(2):
        parent = acc_ref[k * half : (k + 1) * half, :].astype(jnp.bfloat16)
        for c in range(octants):
            leaf = jnp.dot(parent, l2l_ref[c * coeffs : (c + 1) * coeffs, :],
                           preferred_element_type=jnp.float32)
            for p in range(2):
                leaf_ref[p, pl.ds(k * span + c, half, stride=octants), :] = (
                    leaf[:, p * lanes : (p + 1) * lanes])
        for p in range(2):
            sends.append(pltpu.make_async_copy(
                leaf_ref.at[p, pl.ds(k * span, span)],
                out_hbm.at[pl.ds(k * span, span), pl.ds(p * lanes, lanes)], sem.at[2 * k + p]))
            sends[-1].start()
    for send in sends:
        send.wait()


def m2l(table, src, tgt, counts, m2l_ops, l2l, slots, boxes):
    ops = counts.shape[0]
    coeffs = m2l_ops.shape[1]
    chunks_per_op = slots // CHUNK
    chunks = ops * chunks_per_op
    octants = l2l.shape[0] // coeffs
    smem = pl.BlockSpec(memory_space=pltpu.SMEM)
    vmem = pl.BlockSpec(memory_space=pltpu.VMEM)

    def kern(*refs):
        m2l_kernel(ops, chunks_per_op, *refs)

    return pl.pallas_call(
        kern,
        in_specs=[smem, smem, vmem, vmem, vmem, vmem],
        out_specs=pl.BlockSpec(memory_space=pl.ANY),
        out_shape=jax.ShapeDtypeStruct((boxes * octants, coeffs), jnp.float32),
        scratch_shapes=[
            pltpu.VMEM((BATCH * CHUNK, 2, coeffs // 2), jnp.float32),
            pltpu.VMEM((BATCH * CHUNK, coeffs), jnp.bfloat16),
            pltpu.VMEM((boxes, coeffs), jnp.float32),
            pltpu.SMEM((chunks + 4 * BATCH,), jnp.int32),
            pltpu.VMEM((2, boxes * octants, coeffs // 2), jnp.float32),
            pltpu.SemaphoreType.DMA((4,)),
        ],
        compiler_params=pltpu.CompilerParams(vmem_limit_bytes=8 << 20),
        name="m2l",
    )(
        src,
        counts,
        pltpu.with_memory_space_constraint(tgt, pltpu.VMEM),
        pltpu.with_memory_space_constraint(table, pltpu.VMEM),
        pltpu.with_memory_space_constraint(m2l_ops, pltpu.VMEM),
        pltpu.with_memory_space_constraint(l2l, pltpu.VMEM),
    )


def body(
    leaf_multipoles, m2m_ops, m2l_ops, l2l_ops, send_boxes, task_source, task_target, task_count
):
    coeff_count = leaf_multipoles.shape[1]
    box_count = leaf_multipoles.shape[0] // 8
    column = lax.axis_index("gx")
    leaves = leaf_multipoles.reshape(box_count, 8, coeff_count)
    parents = jnp.einsum("bcp,cpq->bq", leaves, m2m_ops, preferred_element_type=jnp.float32).astype(
        jnp.bfloat16
    )
    boxes = send_boxes[0]
    cap = boxes.shape[-1]
    peers = boxes.shape[1]
    other = jnp.where(column == 0, boxes[2], boxes[0])
    lists = jnp.stack([boxes[1], other], 0)
    slots = task_source.shape[2]
    src, tgt = (
        a[0].reshape(-1, 8, slots // CHUNK, CHUNK).transpose(0, 2, 1, 3).reshape(-1, CHUNK)
        for a in (task_source, task_target)
    )
    ops = m2l_ops.reshape(-1, coeff_count)
    l2l = l2l_ops.reshape(-1, coeff_count)
    table, ops, src, tgt, l2l = exchange(parents, lists, ops, src, tgt, l2l)
    return m2l(table, src.reshape(-1), tgt, task_count[0], ops, l2l, slots, box_count)


def solution(mesh):
    return jax.shard_map(
        body,
        mesh=mesh,
        in_specs=(
            P(("gx", "gy"), None),
            P(),
            P(),
            P(),
            P(("gx", "gy"), None, None, None),
            P(("gx", "gy"), None, None),
            P(("gx", "gy"), None, None),
            P(("gx", "gy"), None),
        ),
        out_specs=P(("gx", "gy"), None),
        check_vma=False,
    )
```

```python
import jax
import jax.numpy as jnp
from jax import lax
from jax.experimental import pallas as pl
from jax.experimental.pallas import tpu as pltpu
from jax.sharding import PartitionSpec as P

CHUNK = 128
BATCH = 4
SIDE = 4
UNROLL = 32

INTERNAL = (0, 12, 4, 48, 28, 7, 49, 52, 29, 11, 6, 23, 45, 10, 22, 41, 46, 47)
PARENT = (-1, 0, 6, 7, 0, 6, 7, 4, 12, 10, 6, 7, 0, 29, 10, 12, 0, 29, 22, 23, 4, 22, 23, 7, 28, 41, 22, 11, 12, 28, 29, 47, 48, 49, 46, 47, 52, 41, 22, 23, 41, 45, 41, 47, 45, 29, 45, 46, 0, 48, 49, 48, 48, 52, 6, 7, 52, 41, 10, 11, 12, 49, 46, 47)
PLAN = (
    (0, 0, 0), (0, 0, 1), (1, 0, 0), (1, 0, 1), (1, 0, 16), (0, 12, 0), (0, 4, 0), (0, 48, 0),
    (0, 12, 1), (0, 4, 1), (0, 48, 1), (1, 12, 12), (1, 12, 8), (1, 12, 15), (1, 12, 60),
    (1, 4, 4), (1, 4, 20), (0, 28, 0), (0, 7, 0), (0, 49, 0), (1, 48, 48), (1, 48, 32),
    (1, 48, 51), (0, 52, 0), (0, 28, 1), (0, 7, 1), (0, 49, 1), (1, 28, 28), (1, 28, 24),
    (1, 7, 7), (1, 7, 3), (1, 7, 55), (0, 52, 1), (1, 49, 49), (1, 49, 33), (1, 49, 50),
    (1, 49, 61), (1, 52, 52), (1, 52, 36), (0, 29, 0), (1, 52, 53), (1, 52, 56), (0, 11, 0),
    (0, 29, 1), (0, 6, 0), (0, 23, 0), (1, 29, 29), (1, 29, 13), (1, 29, 17), (1, 29, 30),
    (0, 11, 1), (1, 11, 11), (1, 11, 27), (1, 11, 59), (0, 23, 1), (1, 23, 23), (1, 23, 19),
    (1, 23, 39), (0, 45, 0), (0, 6, 1), (1, 6, 6), (1, 6, 2), (1, 6, 5), (1, 6, 54), (0, 10, 0),
    (0, 45, 1), (0, 22, 0), (1, 45, 45), (1, 45, 44), (0, 41, 0), (0, 46, 0), (0, 22, 1),
    (1, 22, 22), (1, 22, 18), (1, 22, 21), (1, 22, 26), (1, 22, 38), (0, 10, 1), (1, 10, 10),
    (1, 10, 9), (1, 10, 14), (1, 10, 58), (0, 46, 1), (1, 46, 46), (1, 46, 34), (1, 46, 62),
    (0, 41, 1), (1, 41, 41), (1, 41, 25), (1, 41, 37), (0, 47, 0), (1, 41, 40), (1, 41, 42),
    (1, 41, 57), (0, 47, 1), (1, 47, 47), (1, 47, 31), (1, 47, 35), (1, 47, 43), (1, 47, 63),
)

PAD = 4


def list_layout():
    groups, order, pos = {}, [], {}
    for o in INTERNAL:
        members = [o] + [c for c in range(len(PARENT)) if PARENT[c] == o and c not in INTERNAL]
        start = len(order)
        for c in members:
            pos[c] = len(order)
            order.append(c)
        while len(order) % PAD:
            order.append(o)
        groups[o] = (start, len(order) - start)
    return groups, order, pos


def torus_add(base, offset, sign=1):
    parts = []
    for weight in (SIDE * SIDE, SIDE, 1):
        a = lax.rem(lax.div(base, weight), SIDE)
        b = (offset // weight) % SIDE
        if sign < 0:
            b = (SIDE - b) % SIDE
        parts.append(lax.rem(a + b, SIDE) * weight)
    return parts[0] + parts[1] + parts[2]


def comm_kernel(peers, idx_in, own_block, ops_in, src_in, tgt_in, l2l_in, table,
                ops_out, src_out, tgt_out, l2l_out, *scratch):
    blocks = dict(zip(INTERNAL, (own_block,) + scratch[: len(INTERNAL) - 1]))
    scratch = scratch[len(INTERNAL) - 1 :]
    (land, idx, stage_own, stage_other, full_send, full_recv, idx_send, idx_recv, idx_load,
     own_send, own_recv, own_local, other_send, other_recv, keep) = scratch
    groups, order, pos = list_layout()
    slot = {o: i for i, o in enumerate(INTERNAL)}
    cap = stage_own.shape[1]
    boxes = own_block.shape[0]
    half_rows = own_block.shape[0] // 2
    pair = 2 * cap
    me_u = lax.axis_index("gx")
    me_v = lax.axis_index("gy")
    ready = pltpu.get_barrier_semaphore()

    def mesh_id(offset, side=0, sign=1):
        column = me_u if side == 0 else 1 - me_u
        return (column, torus_add(me_v, offset, sign))

    near = [s * w for w in (SIDE * SIDE, SIDE, 1) for s in (1, SIDE - 1)]
    sends = [(o, 0) for o in sorted(set(near) | set(INTERNAL[1:]))]
    sends += [(o, 1) for o in [0] + near]
    for o, side in sends:
        pl.semaphore_signal(ready, inc=1, device_id=mesh_id(o, side, -1),
                            device_id_type=pl.DeviceIdType.MESH)
    pl.semaphore_wait(ready, len(sends))

    def ghost(side, owner, count=1):
        first = boxes + (side * peers + owner) * cap
        return table.at[pl.ds(first, count * cap)]

    def remote(src, dst, send, recv, target):
        return pltpu.make_async_remote_copy(
            src_ref=src, dst_ref=dst, send_sem=send, recv_sem=recv, device_id=target,
            device_id_type=pl.DeviceIdType.MESH,
        )

    def full_copy(child, half):
        parent = PARENT[child]
        rows = pl.ds(half * half_rows, half_rows)
        step = torus_step(parent, child)
        k = (slot[child] - 1) * 2 + half
        return remote(blocks[parent].at[rows], blocks[child].at[rows], full_send.at[k],
                      full_recv.at[k], mesh_id(step))

    def idx_copy(o):
        start, n = groups[o]
        part = pl.ds(start * pair, n * pair)
        return remote(idx_in.at[part], land.at[part], idx_send, idx_recv, mesh_id(o))

    mine = pl.ds(0, groups[0][1] * pair)
    rest = pl.ds(groups[0][1] * pair, (len(order) - groups[0][1]) * pair)
    load_mine = pltpu.make_async_copy(idx_in.at[mine], idx.at[mine], idx_load.at[0])
    load_rest = pltpu.make_async_copy(land.at[rest], idx.at[rest], idx_load.at[1])
    kept = [(own_block, table.at[pl.ds(0, boxes)]), (ops_in, ops_out), (src_in, src_out),
            (tgt_in, tgt_out), (l2l_in, l2l_out)]
    kept = [pltpu.make_async_copy(a, b, keep.at[i]) for i, (a, b) in enumerate(kept)]
    here = (1 - me_u, me_v)
    children = {o: [c for c in INTERNAL if PARENT[c] == o] for o in INTERNAL}
    loaded = set()
    for kind, o, arg in PLAN:
        if kind == 0:
            if o != 0:
                if 0 in loaded and 1 not in loaded:
                    remote(idx_in.at[rest], land.at[rest], idx_send, idx_recv, here).wait_recv()
                    load_rest.start()
                    loaded.add(1)
                full_copy(o, arg).wait_recv()
            for c in children[o]:
                full_copy(c, arg).start()
            if o == 0 and arg == 0:
                load_mine.start()
                for c in INTERNAL[1:]:
                    idx_copy(c).start()
            if o == 0 and arg == 1:
                for copy in kept:
                    copy.start()
            continue
        if o == 0 and 0 not in loaded:
            load_mine.wait()
            loaded.add(0)
        if o != 0 and 2 not in loaded:
            load_rest.wait()
            loaded.add(2)
        block = blocks[o]
        p = pos[arg]

        def pick(g, carry, block=block, p=p):
            for h, stage in ((0, stage_own), (1, stage_other)):
                for i in range(UNROLL):
                    row = block[idx.at[pl.ds(p * pair + h * cap + i, cap)][g * UNROLL]]
                    stage[p, g * UNROLL + i] = row
            return carry

        lax.fori_loop(0, cap // UNROLL, pick, 0)
        owner = torus_add(me_v, o, -1)
        step = torus_step(o, arg) if arg != o else 0
        if arg == o:
            pltpu.make_async_copy(stage_own.at[p], ghost(0, owner), own_local).start()
        else:
            remote(stage_own.at[p], ghost(0, owner), own_send, own_recv, mesh_id(step)).start()
        remote(stage_other.at[p], ghost(1, owner), other_send, other_recv,
               mesh_id(step, 1)).start()

    inner = len(INTERNAL)
    part = ghost(0, 0, peers - inner)
    side = ghost(1, 0, peers)
    remote(part, part, own_send, own_recv, here).wait_recv()
    remote(side, side, other_send, other_recv, here).wait_recv()
    remote(part, part, own_send, own_recv, here).wait_send()
    remote(side, side, other_send, other_recv, here).wait_send()
    part = ghost(0, 0, inner)
    pltpu.make_async_copy(part, part, own_local).wait()
    for copy in kept:
        copy.wait()
    block = peers * cap
    rows = src_out[...]
    first = jnp.logical_and(rows >= boxes, rows < boxes + block)
    moved = jnp.where(jnp.logical_and(me_u == 1, first), rows + block, rows - block)
    rows = jnp.where(rows < boxes, rows, moved)
    src_out[...] = jnp.clip(rows, 0, boxes + 2 * block - 1)
    remote(idx_in.at[rest], land.at[rest], idx_send, idx_recv, here).wait_send()
    for c in INTERNAL[1:]:
        for half in range(2):
            full_copy(c, half).wait_send()


def torus_step(a, b):
    step = 0
    for weight in (SIDE * SIDE, SIDE, 1):
        step += (((b // weight) - (a // weight)) % SIDE) * weight
    return step


def exchange(parents, lists, ops, src, tgt, l2l):
    _, peers, cap = lists.shape
    boxes, coeffs = parents.shape
    groups, order, pos = list_layout()
    me_v = lax.axis_index("gy")
    dest = jnp.stack([torus_add(me_v, o) for o in order])
    idx = jnp.transpose(lists, (1, 0, 2))[dest].reshape(-1)
    inner = len(INTERNAL)
    dma = pltpu.SemaphoreType.DMA
    vmem = pl.BlockSpec(memory_space=pltpu.VMEM)
    anym = pl.BlockSpec(memory_space=pl.ANY)

    def kern(*refs):
        comm_kernel(peers, *refs)

    return pl.pallas_call(
        kern,
        in_specs=[vmem, vmem, anym, anym, anym, anym],
        out_specs=[vmem] * 5,
        out_shape=[
            pltpu.VMEM((boxes + 2 * peers * cap, 2, coeffs // 2), parents.dtype),
            pltpu.VMEM(ops.shape, ops.dtype),
            pltpu.VMEM(src.shape, src.dtype),
            pltpu.VMEM(tgt.shape, tgt.dtype),
            pltpu.VMEM(l2l.shape, l2l.dtype),
        ],
        scratch_shapes=[pltpu.VMEM((boxes, 2, coeffs // 2), parents.dtype)] * (inner - 1)
        + [
            pltpu.VMEM(idx.shape, jnp.int32),
            pltpu.SMEM((idx.shape[0] + 1024,), jnp.int32),
            pltpu.VMEM((len(order), cap, 2, coeffs // 2), parents.dtype),
            pltpu.VMEM((len(order), cap, 2, coeffs // 2), parents.dtype),
            dma((2 * inner - 2,)),
            dma((2 * inner - 2,)),
            dma,
            dma,
            dma((2,)),
            dma, dma, dma, dma, dma,
            dma((5,)),
        ],
        compiler_params=pltpu.CompilerParams(
            collective_id=0, has_side_effects=True, vmem_limit_bytes=20 << 20
        ),
        name="exchange",
    )(idx, parents.reshape(boxes, 2, coeffs // 2),
      *(pltpu.with_memory_space_constraint(a, pltpu.HBM) for a in (ops, src, tgt, l2l)))


def m2l_kernel(ops, chunks_per_op, src_ref, count_ref, tgt_ref, tab_ref, op_ref, l2l_ref, out_hbm,
               x_ref, y_ref, acc_ref, list_ref, leaf_ref, sem):
    boxes, coeffs = acc_ref.shape
    size = src_ref.shape[0]
    empty = size
    acc_ref[...] = jnp.zeros_like(acc_ref)
    y_ref[...] = jnp.zeros_like(y_ref)

    def fill(o, pos):
        n = lax.div(count_ref[o] + (CHUNK - 1), CHUNK)
        first = lax.div(o, 8) * (8 * CHUNK * chunks_per_op) + lax.rem(o, 8) * CHUNK
        for c in range(chunks_per_op):
            list_ref[pos] = first + c * (8 * CHUNK)
            pos = pos + jnp.where(c < n, 1, 0)
        return pos

    def locate(first):
        o = lax.div(first, 8 * CHUNK * chunks_per_op) * 8 + lax.rem(lax.div(first, CHUNK), 8)
        c = lax.rem(lax.div(first, 8 * CHUNK), chunks_per_op)
        return jnp.minimum(o, ops - 1), c

    for i in range(BATCH):
        list_ref[i] = empty
    total = lax.fori_loop(0, ops, fill, BATCH)
    for i in range(3 * BATCH):
        list_ref[total + i] = empty

    def gather(it):
        for h in range(BATCH):
            first = list_ref[BATCH * it + h]
            first = jnp.where(first < empty, first, 0)
            for i in range(CHUNK):
                s = src_ref.at[pl.ds(i, size - CHUNK + 1)][first]
                x_ref[h * CHUNK + i] = tab_ref[s].astype(jnp.float32)

    def translate(it):
        x2 = x_ref.reshape(2 * BATCH * CHUNK, x_ref.shape[2])
        for h in range(BATCH):
            o, _ = locate(list_ref[BATCH * it + h])
            first = 2 * CHUNK * h
            lo = x2[pl.ds(first, CHUNK, stride=2), :].astype(jnp.bfloat16)
            hi = x2[pl.ds(first + 1, CHUNK, stride=2), :].astype(jnp.bfloat16)
            w = op_ref[pl.ds(pl.multiple_of(o * coeffs, coeffs), coeffs), :]
            y_ref[h * CHUNK : (h + 1) * CHUNK, :] = jnp.dot(
                jnp.concatenate([lo, hi], axis=1), w, preferred_element_type=jnp.float32
            ).astype(jnp.bfloat16)

    def scatter(it):
        rows = lax.broadcasted_iota(jnp.int32, (boxes, CHUNK), 0)
        ps = []
        for h in range(BATCH):
            first = list_ref[BATCH * it + h]
            o, c = locate(first)
            used = jnp.where(first < empty, count_ref[o] - c * CHUNK, 0)
            first = jnp.where(first < empty, first, 0)
            t = tgt_ref[pl.ds(lax.div(first, CHUNK), 1), :]
            t = jnp.where(lax.broadcasted_iota(jnp.int32, (1, CHUNK), 1) < used, t, -1)
            ps.append(jnp.where(rows == t, 1.0, 0.0).astype(jnp.bfloat16))
        acc_ref[...] += jnp.dot(
            jnp.concatenate(ps, axis=1), y_ref[...], preferred_element_type=jnp.float32
        )

    gather(1)

    @pl.loop(1, lax.div(total + BATCH - 1, BATCH) + 1)
    def _(j):
        scatter(j - 1)
        translate(j)
        gather(j + 1)

    half = boxes // 2
    octants = l2l_ref.shape[0] // coeffs
    span = half * octants
    lanes = leaf_ref.shape[2]
    sends = []
    for k in range(2):
        parent = acc_ref[k * half : (k + 1) * half, :].astype(jnp.bfloat16)
        for c in range(octants):
            leaf = jnp.dot(parent, l2l_ref[c * coeffs : (c + 1) * coeffs, :],
                           preferred_element_type=jnp.float32)
            for p in range(2):
                leaf_ref[p, pl.ds(k * span + c, half, stride=octants), :] = (
                    leaf[:, p * lanes : (p + 1) * lanes])
        for p in range(2):
            sends.append(pltpu.make_async_copy(
                leaf_ref.at[p, pl.ds(k * span, span)],
                out_hbm.at[pl.ds(k * span, span), pl.ds(p * lanes, lanes)], sem.at[2 * k + p]))
            sends[-1].start()
    for send in sends:
        send.wait()


def m2l(table, src, tgt, counts, m2l_ops, l2l, slots, boxes):
    ops = counts.shape[0]
    coeffs = m2l_ops.shape[1]
    chunks_per_op = slots // CHUNK
    chunks = ops * chunks_per_op
    octants = l2l.shape[0] // coeffs
    smem = pl.BlockSpec(memory_space=pltpu.SMEM)
    vmem = pl.BlockSpec(memory_space=pltpu.VMEM)

    def kern(*refs):
        m2l_kernel(ops, chunks_per_op, *refs)

    return pl.pallas_call(
        kern,
        in_specs=[smem, smem, vmem, vmem, vmem, vmem],
        out_specs=pl.BlockSpec(memory_space=pl.ANY),
        out_shape=jax.ShapeDtypeStruct((boxes * octants, coeffs), jnp.float32),
        scratch_shapes=[
            pltpu.VMEM((BATCH * CHUNK, 2, coeffs // 2), jnp.float32),
            pltpu.VMEM((BATCH * CHUNK, coeffs), jnp.bfloat16),
            pltpu.VMEM((boxes, coeffs), jnp.float32),
            pltpu.SMEM((chunks + 4 * BATCH,), jnp.int32),
            pltpu.VMEM((2, boxes * octants, coeffs // 2), jnp.float32),
            pltpu.SemaphoreType.DMA((4,)),
        ],
        compiler_params=pltpu.CompilerParams(vmem_limit_bytes=8 << 20),
        name="m2l",
    )(
        src,
        counts,
        pltpu.with_memory_space_constraint(tgt, pltpu.VMEM),
        pltpu.with_memory_space_constraint(table, pltpu.VMEM),
        pltpu.with_memory_space_constraint(m2l_ops, pltpu.VMEM),
        pltpu.with_memory_space_constraint(l2l, pltpu.VMEM),
    )


def body(
    leaf_multipoles, m2m_ops, m2l_ops, l2l_ops, send_boxes, task_source, task_target, task_count
):
    coeff_count = leaf_multipoles.shape[1]
    box_count = leaf_multipoles.shape[0] // 8
    column = lax.axis_index("gx")
    leaves = leaf_multipoles.reshape(box_count, 8, coeff_count)
    parents = jnp.einsum("bcp,cpq->bq", leaves, m2m_ops, preferred_element_type=jnp.float32).astype(
        jnp.bfloat16
    )
    boxes = send_boxes[0]
    cap = boxes.shape[-1]
    peers = boxes.shape[1]
    other = jnp.where(column == 0, boxes[2], boxes[0])
    lists = jnp.stack([boxes[1], other], 0)
    slots = task_source.shape[2]
    src, tgt = (
        a[0].reshape(-1, 8, slots // CHUNK, CHUNK).transpose(0, 2, 1, 3).reshape(-1, CHUNK)
        for a in (task_source, task_target)
    )
    ops = m2l_ops.reshape(-1, coeff_count)
    l2l = l2l_ops.reshape(-1, coeff_count)
    table, ops, src, tgt, l2l = exchange(parents, lists, ops, src, tgt, l2l)
    return m2l(table, src.reshape(-1), tgt, task_count[0], ops, l2l, slots, box_count)


def solution(mesh):
    return jax.shard_map(
        body,
        mesh=mesh,
        in_specs=(
            P(("gx", "gy"), None),
            P(),
            P(),
            P(),
            P(("gx", "gy"), None, None, None),
            P(("gx", "gy"), None, None),
            P(("gx", "gy"), None, None),
            P(("gx", "gy"), None),
        ),
        out_specs=P(("gx", "gy"), None),
        check_vma=False,
    )
```
